128 devices in a mesh: tm: 16 (over z, y), seq: 8 (over x, core).
Axes of the slice: x: 4, y: 4, z: 4, core: 2. Of those that a mesh axis runs over, the one named last changes fastest.
Arguments:
- latents: float32 [16, 1536, 3072], P('tm', 'seq'), may hold values from -6 to 6
- timesteps: int32 [17], replicated, may hold values from 1 to 999, as said below
- mod_weight: bfloat16 [256, 9216], replicated, may hold values from -0.375 to 0.375
- qkv_weight: bfloat16 [3, 3072, 3072], P(None, None, 'seq'), may hold values from -0.109375 to 0.109375
- qk_gain: float32 [2, 128], replicated, may hold values from 1 to 3
- out_weight: bfloat16 [3072, 3072], P('seq'), may hold values from -0.109375 to 0.109375
- block_list: int32 [24, 4, 3], P('seq'), may hold values from 0 to 3, as said below
Outputs:
- updated: float32 [16, 1536, 3072], P('tm', 'seq')
The draws below stay inside these ranges and needn't reach their ends.
Inputs may be any that keep to these rules, and one draw needn't show every extreme that they name: `timesteps`: strictly falling, first entry 999, last entry 1. `block_list`: each row names 3 different key tiles, the first being the query tile itself.
All inputs are finite; a program needn't handle non-finite values.
Results may differ from the reference program's by a relative error of at most 0.008.
Values may be sent and summed in bfloat16 or wider, within the bound.
No kernel may reach another device: no remote copies, remote signals or barrier semaphores. Data moves between devices by JAX's collectives and lax.ppermute only.
A program may use at most 128 MiB of HBM per device.

```python
import math
import jax
import jax.numpy as jnp
from jax import lax

D = 3072
HEADS = 24
HEAD_DIM = 128
FREQ = 256
BLOCK = 384
KEEP = 3
STEPS = 16
TOKENS = 1536


def draw_timesteps(key, part):
    key = jax.random.fold_in(key, 11)
    widths = jax.random.randint(key, (STEPS,), 1, 9).astype(jnp.int32)
    running = jnp.concatenate([jnp.zeros((1,), jnp.int32), jnp.cumsum(widths).astype(jnp.int32)])
    total = running[-1]
    return (999 - running * 998 // total).astype(jnp.int32)


def draw_block_list(key, part):
    key = jax.random.fold_in(key, 23)
    nblk = TOKENS // BLOCK
    noise = jax.random.randint(key, (HEADS, nblk, nblk), 0, 1 << 16).astype(jnp.int32)
    scores = noise * nblk + jnp.arange(nblk, dtype=jnp.int32)[None, None, :]
    diagonal = jnp.arange(nblk)[:, None] == jnp.arange(nblk)[None, :]
    scores = jnp.where(diagonal[None], jnp.int32(1 << 30), scores)
    return lax.top_k(scores, KEEP)[1].astype(jnp.int32)


def draw_qk_gain(key, part):
    key = jax.random.fold_in(key, 37)
    values = jnp.exp(jax.random.uniform(key, (2, HEAD_DIM), jnp.float32, jnp.log(1.2), jnp.log(2.5)))
    return values


def block_levels(own_key, extent, cuts, low, high):
    loudness = 1.0
    for axis_at, parts in cuts:
        steps = jax.random.uniform(jax.random.fold_in(jax.random.fold_in(own_key, 6), axis_at), (parts,), jnp.float32, low / len(cuts), high / len(cuts))
        loudness = loudness * jnp.repeat(jnp.exp(steps), extent[axis_at] // parts).reshape((-1,) + (1,) * (len(extent) - 1 - axis_at))
    return loudness


def bell_draw(own_key, dims, scale, bound, cuts=(), kind=jnp.bfloat16):
    values = scale * jax.random.normal(own_key, dims, jnp.float32)
    if cuts:
        values = values * block_levels(own_key, dims, cuts, -0.22, 0.18)
    return jnp.clip(values, -bound, bound).astype(kind)


def setup_inputs(seed: int = 0) -> dict:
    seeds = jax.random.split(jax.random.key(seed), 8)
    return {
        "latents": bell_draw(seeds[0], (STEPS, TOKENS, D), 1.0, 6.0, ((0, 16), (1, 8)), jnp.float32),
        "timesteps": draw_timesteps(jax.random.fold_in(seeds[7], 71), 0),
        "mod_weight": bell_draw(seeds[2], (FREQ, 3 * D), FREQ ** -0.5, 0.375),
        "qkv_weight": bell_draw(seeds[3], (3, D, D), D ** -0.5, 0.109375, ((2, 8),)),
        "qk_gain": draw_qk_gain(jax.random.fold_in(seeds[7], 71), 0),
        "out_weight": bell_draw(seeds[5], (D, D), D ** -0.5, 0.109375, ((0, 8),)),
        "block_list": draw_block_list(jax.random.fold_in(seeds[7], 71), 0),
    }


eps_norm = 1e-06

def embed(stamp, freq_dim):
    half = freq_dim // 2
    freqs = jnp.exp(-jnp.log(10000.0) * jnp.arange(half, dtype=jnp.float32) / half)
    angles = stamp.astype(jnp.float32) * freqs
    return jnp.concatenate([jnp.cos(angles), jnp.sin(angles)]).astype(jnp.bfloat16)

def modulate(current, stamp, mod_weight):
    emb = embed(stamp, mod_weight.shape[0])
    mod = jnp.dot(emb[None, :], mod_weight, preferred_element_type=jnp.float32)[0]
    width = current.shape[-1]
    shift = mod[:width]
    scale = mod[width:2 * width]
    gate = mod[2 * width:]
    mean = lax.optimization_barrier(jnp.mean(current, axis=-1, keepdims=True))
    centred = current - mean
    var = lax.optimization_barrier(jnp.mean(centred * centred, axis=-1, keepdims=True))
    normed = centred * lax.rsqrt(var + eps_norm)
    return ((normed * (1.0 + scale) + shift).astype(jnp.bfloat16), gate)

def head_norm(proj, gain, head_dim):
    count = proj.shape[0]
    split = proj.reshape(count, -1, head_dim)
    inverse = lax.rsqrt(lax.optimization_barrier(jnp.mean(split * split, axis=-1, keepdims=True)) + eps_norm)
    return (split * inverse * gain).reshape(count, -1).astype(jnp.bfloat16)

def project(source, qkv_weight, qk_gain):
    head_dim = qk_gain.shape[1]
    query = jnp.dot(source, qkv_weight[0], preferred_element_type=jnp.float32)
    keyset = jnp.dot(source, qkv_weight[1], preferred_element_type=jnp.float32)
    valset = jnp.dot(source, qkv_weight[2], preferred_element_type=jnp.float32)
    return (head_norm(query, qk_gain[0], head_dim), head_norm(keyset, qk_gain[1], head_dim), valset.astype(jnp.bfloat16))

def attend(query, keyset, valset, block_list, head_dim, block):
    tokens = query.shape[0]
    heads = query.shape[1] // head_dim
    nblk = tokens // block

    def arrange(x):
        return x.reshape(nblk, block, heads, head_dim).transpose(2, 0, 1, 3)
    q_heads = arrange(query).astype(jnp.float32)
    k_heads = arrange(keyset)
    v_heads = arrange(valset)
    picker = jax.vmap(lambda tiles, idx: tiles[idx])
    k_sel = picker(k_heads, block_list).reshape(heads, nblk, -1, head_dim).astype(jnp.float32)
    v_sel = picker(v_heads, block_list).reshape(heads, nblk, -1, head_dim).astype(jnp.float32)
    scores = jnp.einsum('hqbd,hqkd->hqbk', q_heads, k_sel) / math.sqrt(head_dim)
    weights = jax.nn.softmax(scores, axis=-1)
    probs = weights.astype(jnp.bfloat16).astype(jnp.float32)
    result = jnp.einsum('hqbk,hqkd->hqbd', probs, v_sel).astype(jnp.bfloat16)
    return result.transpose(1, 2, 0, 3).reshape(tokens, heads * head_dim)

def reference(latents, timesteps, mod_weight, qkv_weight, qk_gain, out_weight, block_list):
    head_dim = qk_gain.shape[1]

    def one_step(step):
        current = latents[step]
        modulated, gate = modulate(current, timesteps[step], mod_weight)
        query, keyset, valset = project(modulated, qkv_weight, qk_gain)
        attended = attend(query, keyset, valset, block_list, head_dim, BLOCK)
        drift = gate * jnp.dot(attended, out_weight, preferred_element_type=jnp.float32)
        delta = (timesteps[step + 1] - timesteps[step]).astype(jnp.float32) / 1000.0
        return delta * drift
    terms = lax.map(one_step, jnp.arange(STEPS, dtype=jnp.int32))
    terms = terms.at[0].add(latents[0])
    return jnp.cumsum(terms, axis=0)
```

```python
import functools
import math

import jax
import jax.numpy as jnp
from jax import lax
from jax.experimental import pallas as pl
from jax.experimental.pallas import tpu as pltpu
from jax.sharding import PartitionSpec as P

D = 3072
BLOCK = 384
HEAD = 128
LOCAL_HEADS = 3
WIDTH = LOCAL_HEADS * HEAD
NX = 4
NY = 4
NZ = 4
ROWS = 192
SUB = 48
COLS = D // NY
DEEP = WIDTH // NZ
eps_norm = 1e-06

BF = jnp.bfloat16
F32 = jnp.float32


def embed(stamp, freq_dim):
    half = freq_dim // 2
    freqs = jnp.exp(-jnp.log(10000.0) * jnp.arange(half, dtype=F32) / half)
    angles = stamp.astype(F32) * freqs
    return jnp.concatenate([jnp.cos(angles), jnp.sin(angles)]).astype(BF)


def modulate(current, stamp, mod_weight):
    emb = embed(stamp, mod_weight.shape[0])
    mod = jnp.dot(emb[None, :], mod_weight[:, : 2 * D], preferred_element_type=F32)[0]
    shift = mod[:D]
    scale = mod[D:]
    mean = jnp.mean(current, axis=-1, keepdims=True)
    centred = current - mean
    var = jnp.mean(centred * centred, axis=-1, keepdims=True)
    normed = centred * lax.rsqrt(var + eps_norm)
    return (normed * (1.0 + scale) + shift).astype(BF)


def shift_x(array, by):
    return lax.ppermute(array, "seq", [(i, (i + 2 * by) % 8) for i in range(8)])


def swap_core(array):
    return lax.ppermute(array, "seq", [(i, i ^ 1) for i in range(8)])


def shift_y(array, by):
    pairs = [(z * NY + y, z * NY + (y + by) % NY) for z in range(NZ) for y in range(NY)]
    return lax.ppermute(array, "tm", pairs)


def up_z(array, by):
    pairs = [(z * NY + y, (z + by) * NY + y) for z in range(NZ - by) for y in range(NY)]
    return lax.ppermute(array, "tm", pairs)


def qkv_kernel(parts, *refs):
    ins = refs[:parts]
    gain_ref, w_ref, _, out_ref, rows, sems = refs[parts:]
    kind = pl.program_id(0)

    @pl.when(kind == 0)
    def _():
        copies = []
        at = 0
        for n, part in enumerate(ins):
            size = part.shape[0]
            copies.append(pltpu.make_async_copy(part, rows.at[pl.ds(at, size)], sems.at[n]))
            at += size
        for copy in copies:
            copy.start()
        for copy in copies:
            copy.wait()

    proj = jnp.dot(rows[...], w_ref[0], preferred_element_type=F32)

    @pl.when(kind < 2)
    def _():
        gain = gain_ref[pl.ds(kind, 1), :]
        for h in range(LOCAL_HEADS):
            cols = slice(h * HEAD, (h + 1) * HEAD)
            part = proj[:, cols]
            inverse = lax.rsqrt(jnp.mean(part * part, axis=-1, keepdims=True) + eps_norm)
            out_ref[0, 0, :, cols] = (part * inverse * gain).astype(BF)

    @pl.when(kind == 2)
    def _():
        out_ref[0, 0] = proj.astype(BF)


def qkv_tile(parts, place, gain, weight, held):
    n = len(parts)
    return pl.pallas_call(
        functools.partial(qkv_kernel, n),
        grid=(3,),
        in_specs=[pl.BlockSpec(memory_space=pl.ANY)] * n
        + [
            pl.BlockSpec((2, HEAD), lambda i: (0, 0)),
            pl.BlockSpec((1, D, WIDTH), lambda i: (i, 0, 0)),
            pl.BlockSpec(memory_space=pl.ANY),
        ],
        out_specs=pl.BlockSpec((1, 1, BLOCK, WIDTH), lambda i: (i, place, 0, 0)),
        out_shape=jax.ShapeDtypeStruct((3, NX, BLOCK, WIDTH), BF),
        scratch_shapes=[pltpu.VMEM((BLOCK, D), BF), pltpu.SemaphoreType.DMA((n,))],
        input_output_aliases={n + 2: 0},
        compiler_params=pltpu.CompilerParams(vmem_limit_bytes=32 << 20),
        cost_estimate=pl.CostEstimate(
            flops=2 * BLOCK * D * 3 * WIDTH, bytes_accessed=10_000_000, transcendentals=0
        ),
        name="qkv_tile",
    )(*parts, gain, weight, held)


def attend_kernel(list_ref, q_ref, k_ref, v_ref, out_ref):
    head = pl.program_id(0)
    factor = math.log2(math.e) / math.sqrt(HEAD)
    query = q_ref[0, 0]
    tiles = [list_ref[head * 3 + n] for n in range(3)]
    scores = [
        lax.dot_general(query, k_ref[0, t], (((1,), (1,)), ((), ())), preferred_element_type=F32)
        for t in tiles
    ]
    top = functools.reduce(jnp.maximum, [jnp.max(s, axis=-1, keepdims=True) for s in scores])
    total = jnp.zeros((BLOCK, 2 * HEAD), F32)
    ones = jnp.ones((BLOCK, HEAD), BF)
    for s, t in zip(scores, tiles):
        probs = jnp.exp2((s - top) * factor).astype(BF)
        total += jnp.dot(probs, jnp.concatenate([v_ref[0, t], ones], axis=1), preferred_element_type=F32)
    out_ref[...] = (total[:, :HEAD] / total[:, HEAD:]).astype(BF)


def attend_tile(key_tiles, place, held):
    def tile(kind):
        return pl.BlockSpec((1, NX, BLOCK, HEAD), lambda h, t, kind=kind: (kind, 0, 0, h))

    return pl.pallas_call(
        attend_kernel,
        grid_spec=pltpu.PrefetchScalarGridSpec(
            num_scalar_prefetch=1,
            grid=(LOCAL_HEADS,),
            in_specs=[
                pl.BlockSpec((1, 1, BLOCK, HEAD), lambda h, t: (0, place, 0, h)),
                tile(1),
                tile(2),
            ],
            out_specs=pl.BlockSpec((BLOCK, HEAD), lambda h, t: (0, h)),
        ),
        out_shape=jax.ShapeDtypeStruct((BLOCK, WIDTH), BF),
        compiler_params=pltpu.CompilerParams(vmem_limit_bytes=32 << 20),
        cost_estimate=pl.CostEstimate(
            flops=4 * 3 * BLOCK * 3 * BLOCK * HEAD * 2,
            bytes_accessed=3_000_000,
            transcendentals=3 * BLOCK * 3 * BLOCK,
        ),
        name="attend_tile",
    )(key_tiles, held, held, held)


def out_kernel(a0, a1, a2, a3, own_ref, w_ref, out_ref):
    acc = jnp.zeros((ROWS, COLS), F32)
    for d in range(NX):
        rows = jnp.concatenate([a[d, 0] for a in (a0, a1, a2, a3)], axis=0)
        weight = own_ref[...] if d == 0 else w_ref[:, 0, d - 1].reshape(WIDTH, COLS)
        acc += jnp.dot(rows, weight, preferred_element_type=F32)
    out_ref[...] = acc.astype(out_ref.dtype)


def out_half(pieces, half, own, gathered, dtype):
    piece = pl.BlockSpec((NX, 1, SUB, WIDTH), lambda n: (0, half, 0, 0))
    return pl.pallas_call(
        out_kernel,
        grid=(NY,),
        in_specs=[piece] * 4
        + [
            pl.BlockSpec((WIDTH, COLS), lambda n: (0, n)),
            pl.BlockSpec((NZ, 1, NX - 1, DEEP, COLS), lambda n: (0, n, 0, 0, 0)),
        ],
        out_specs=pl.BlockSpec((ROWS, COLS), lambda n: (0, n)),
        out_shape=jax.ShapeDtypeStruct((ROWS, D), dtype),
        compiler_params=pltpu.CompilerParams(vmem_limit_bytes=32 << 20),
        cost_estimate=pl.CostEstimate(
            flops=2 * ROWS * NX * WIDTH * D, bytes_accessed=12_000_000, transcendentals=0
        ),
        name="out_half",
    )(*pieces, own, gathered)


def row_kernel(order_ref, own_ref, other_ref, gate_ref, part_ref, total_ref, held):
    for d in range(NY):
        term = own_ref[d] + other_ref[d].astype(F32)
        held[order_ref[d]] = gate_ref[pl.ds(d, 1), :] * term
    held[1] = held[0] + held[1]
    held[2] = held[1] + held[2]
    held[3] = held[2] + held[3]
    total_ref[...] = held[3].astype(BF)
    for d in range(NY):
        part_ref[d] = held[order_ref[d]]


def row_prefix(order, own, other, gates):
    cols = D // 4
    return pl.pallas_call(
        row_kernel,
        grid_spec=pltpu.PrefetchScalarGridSpec(
            num_scalar_prefetch=1,
            grid=(4,),
            in_specs=[
                pl.BlockSpec((NY, SUB, cols), lambda n, o: (0, 0, n)),
                pl.BlockSpec((NY, SUB, cols), lambda n, o: (0, 0, n)),
                pl.BlockSpec((NY, cols), lambda n, o: (0, n)),
            ],
            out_specs=[
                pl.BlockSpec((NY, SUB, cols), lambda n, o: (0, 0, n)),
                pl.BlockSpec((SUB, cols), lambda n, o: (0, n)),
            ],
            scratch_shapes=[pltpu.VMEM((NY, SUB, cols), F32)],
        ),
        out_shape=[
            jax.ShapeDtypeStruct((NY, SUB, D), F32),
            jax.ShapeDtypeStruct((SUB, D), BF),
        ],
        compiler_params=pltpu.CompilerParams(vmem_limit_bytes=32 << 20),
        cost_estimate=pl.CostEstimate(flops=8 * ROWS * D, bytes_accessed=6_000_000, transcendentals=0),
        name="row_prefix",
    )(order, own.reshape(NY, SUB, D), other.reshape(NY, SUB, D), gates)


def final_kernel(place_ref, lat_ref, p0, p1, p2, p3, out_ref):
    n = pl.program_id(0)
    for d, piece in enumerate((p0, p1, p2, p3)):

        @pl.when(n == d)
        def _(piece=piece):
            out_ref[0] = lat_ref[0] + piece[...].astype(F32)


def final_sum(place, lat, pieces):
    piece = pl.BlockSpec((SUB, D), lambda n, o: (0, 0))
    block = pl.BlockSpec((1, SUB, D), lambda n, o: (o[n], 0, 0))
    return pl.pallas_call(
        final_kernel,
        grid_spec=pltpu.PrefetchScalarGridSpec(
            num_scalar_prefetch=1,
            grid=(NY,),
            in_specs=[block, piece, piece, piece, piece],
            out_specs=block,
        ),
        out_shape=jax.ShapeDtypeStruct((NY, SUB, D), F32),
        compiler_params=pltpu.CompilerParams(vmem_limit_bytes=32 << 20),
        cost_estimate=pl.CostEstimate(flops=ROWS * D, bytes_accessed=6_000_000, transcendentals=0),
        name="final_sum",
    )(place, lat.reshape(NY, SUB, D), *pieces)


def first_latents(current, step, y):
    half = current.astype(jnp.float16)
    mine = half[:SUB]
    for to in range(1, NY):
        got = lax.ppermute(half[to * SUB : (to + 1) * SUB], "tm", [(0, to)])
        mine = jnp.where(y == to, got, mine)
    part = mine[:, :COLS]
    for to in range(1, NZ):
        got = lax.ppermute(
            mine[:, to * COLS : (to + 1) * COLS], "tm", [(n, to * NY + n) for n in range(NY)]
        )
        part = jnp.where(step // NY == to, got, part)
    whole = lax.all_gather(part, "tm").reshape(NZ, NY, SUB, COLS)
    whole = whole.transpose(1, 2, 0, 3).reshape(ROWS, D).astype(F32)
    return jnp.where(step == 0, current, whole)


def per_device(latents, timesteps, mod_weight, qkv_weight, qk_gain, out_weight, block_list):
    step = lax.axis_index("tm")
    z, y = step // NY, step % NY
    x = lax.axis_index("seq") // 2
    current = latents[0]

    piece = lax.dynamic_slice(out_weight, (z * DEEP, y * COLS), (DEEP, COLS))
    piece = jnp.stack([shift_x(piece, d) for d in range(1, NX)])
    gathered = lax.all_gather(piece, "tm").reshape(NZ, NY, NX - 1, DEEP, COLS)

    stamp = lax.dynamic_index_in_dim(timesteps, step, 0, keepdims=False)
    modulated = modulate(current, stamp, mod_weight)

    twin = swap_core(modulated)
    before = shift_x(modulated, 1)
    after = shift_x(modulated, -1)
    far_top = shift_x(before[: ROWS // 2], 1)
    far_low = shift_x(after[ROWS // 2 :], -1)
    held = jnp.zeros((3, NX, BLOCK, WIDTH), BF)
    held = qkv_tile([modulated, twin], 0, qk_gain, qkv_weight, held)
    held = qkv_tile([after, swap_core(after)], 1, qk_gain, qkv_weight, held)
    held = qkv_tile([before, swap_core(before)], 3, qk_gain, qkv_weight, held)
    held = qkv_tile(
        [far_top, far_low, swap_core(far_top), swap_core(far_low)], 2, qk_gain, qkv_weight, held
    )

    tiles = (block_list - x) % NX
    arrived = [None] * NX
    for d in (2, 1, 3, 0):
        key_tiles = lax.dynamic_index_in_dim(tiles, (x + d) % NX, 1, keepdims=False).reshape(-1)
        attended = attend_tile(key_tiles, d, held)
        arrived[d] = shift_x(attended, d) if d else attended
    rows = jnp.stack(arrived).reshape(NX, 2, NY, SUB, WIDTH)

    pieces = []
    for d in range(NY):
        send = lax.dynamic_index_in_dim(rows, (y + d) % NY, 2, keepdims=False)
        pieces.append(shift_y(send, d) if d else send)

    other = swap_core(out_half(pieces, 1, out_weight, gathered, BF))
    own = out_half(pieces, 0, out_weight, gathered, F32)

    order = (y - jnp.arange(NY, dtype=jnp.int32)) % NY
    stamps = z * NY + order
    row_emb = jax.vmap(lambda s: embed(s, mod_weight.shape[0]))(timesteps[stamps])
    gates = jnp.dot(row_emb, mod_weight[:, 2 * D :], preferred_element_type=F32)
    delta = (timesteps[stamps + 1] - timesteps[stamps]).astype(F32) / 1000.0
    parts, total = row_prefix(order, own, other, gates * delta[:, None])
    base = sum(up_z(total, by).astype(F32) for by in range(1, NZ))

    back = []
    for d in range(NY):
        send = (parts[d] + base).astype(BF)
        back.append(shift_y(send, -d) if d else send)
    place = (y + jnp.arange(NY, dtype=jnp.int32)) % NY
    lat = first_latents(current, step, y)
    return final_sum(place, lat, back).reshape(1, ROWS, D)


def solution(mesh):
    return jax.shard_map(
        per_device,
        mesh=mesh,
        in_specs=(
            P("tm", "seq", None),
            P(),
            P(),
            P(None, None, "seq"),
            P(),
            P("seq", None),
            P("seq", None, None),
        ),
        out_specs=P("tm", "seq", None),
        check_vma=False,
    )
```

```python
import functools
import math

import jax
import jax.numpy as jnp
from jax import lax
from jax.experimental import pallas as pl
from jax.experimental.pallas import tpu as pltpu
from jax.sharding import PartitionSpec as P

D = 3072
BLOCK = 384
HEAD = 128
LOCAL_HEADS = 3
WIDTH = LOCAL_HEADS * HEAD
NX = 4
NY = 4
NZ = 4
ROWS = 192
SUB = 48
COLS = D // NY
DEEP = WIDTH // NZ
eps_norm = 1e-06

BF = jnp.bfloat16
F32 = jnp.float32
VMEM = pl.BlockSpec(memory_space=pltpu.VMEM)
SMEM = pl.BlockSpec(memory_space=pltpu.SMEM)


def modulate_kernel(stamps_ref, freq_ref, w_hbm, lat_hbm, out_ref, gate_ref, w, lat, held, w_sems, lat_sems):
    step = lax.axis_index("tm")
    row, y = step // NY, step % NY
    lat_copies = [
        pltpu.make_async_copy(lat_hbm.at[0, part], lat.at[part], lat_sems.at[n])
        for n, part in enumerate(pl.ds(n * SUB, SUB) for n in range(4))
    ]
    w_copies = [
        pltpu.make_async_copy(w_hbm.at[:, part], w.at[:, part], w_sems.at[n])
        for n, part in enumerate(pl.ds(n * D, D) for n in range(3))
    ]
    for copy in lat_copies[:1] + w_copies[:2] + lat_copies[1:] + w_copies[2:]:
        copy.start()

    lane = lax.broadcasted_iota(jnp.int32, (8, HEAD), 0)
    stamps = jnp.zeros((8, HEAD), F32)
    for n in range(NY):
        stamps = jnp.where(lane == n, stamps_ref[row * NY + n].astype(F32), stamps)
    angles = stamps * freq_ref[...]
    emb = jnp.concatenate([jnp.cos(angles), jnp.sin(angles)], axis=1).astype(BF)

    def project(n):
        w_copies[n].wait()
        held[:, n * D : (n + 1) * D] = jnp.dot(
            emb, w[:, n * D : (n + 1) * D], preferred_element_type=F32
        )

    project(0)
    project(1)
    shift = held[pl.ds(y, 1), :D]
    scale = held[pl.ds(y, 1), D : 2 * D]
    for n in range(4):
        lat_copies[n].wait()
        part = slice(n * SUB, (n + 1) * SUB)
        current = lat[part, :]
        centred = current - jnp.mean(current, axis=-1, keepdims=True)
        var = jnp.mean(centred * centred, axis=-1, keepdims=True)
        normed = centred * lax.rsqrt(var + eps_norm)
        out_ref[part, :] = (normed * (1.0 + scale) + shift).astype(BF)
    project(2)
    for n in range(NY):
        delta = (stamps_ref[row * NY + n + 1] - stamps_ref[row * NY + n]).astype(F32) / 1000.0
        gate_ref[n : n + 1, :] = held[n : n + 1, 2 * D :] * delta


def modulate(latents, timesteps, mod_weight):
    half = mod_weight.shape[0] // 2
    freqs = jnp.exp(-jnp.log(10000.0) * jnp.arange(half, dtype=F32) / half)
    return pl.pallas_call(
        modulate_kernel,
        in_specs=[
            pl.BlockSpec(memory_space=pltpu.SMEM),
            VMEM,
            pl.BlockSpec(memory_space=pl.ANY),
            pl.BlockSpec(memory_space=pl.ANY),
        ],
        out_specs=[VMEM, VMEM],
        out_shape=[
            jax.ShapeDtypeStruct((ROWS, D), BF),
            jax.ShapeDtypeStruct((NY, D), F32),
        ],
        scratch_shapes=[
            pltpu.VMEM((2 * half, 3 * D), BF),
            pltpu.VMEM((ROWS, D), F32),
            pltpu.VMEM((8, 3 * D), F32),
            pltpu.SemaphoreType.DMA((3,)),
            pltpu.SemaphoreType.DMA((4,)),
        ],
        compiler_params=pltpu.CompilerParams(vmem_limit_bytes=58 << 20),
        cost_estimate=pl.CostEstimate(flops=1, bytes_accessed=1, transcendentals=0),
        name="modulate",
    )(timesteps, freqs[None], mod_weight, latents)


def shift_x(array, by):
    return lax.ppermute(array, "seq", [(i, (i + 2 * by) % 8) for i in range(8)])


def swap_core(array):
    return lax.ppermute(array, "seq", [(i, i ^ 1) for i in range(8)])


def shift_y(array, by):
    pairs = [(z * NY + y, z * NY + (y + by) % NY) for z in range(NZ) for y in range(NY)]
    return lax.ppermute(array, "tm", pairs)


def opposite_x(forward, backward):
    core = lax.axis_index("seq") % 2
    send = jnp.where(core == 0, forward, backward)
    return lax.ppermute(send, "seq", [(i, (i + 2 - 4 * (i % 2)) % 8) for i in range(8)])


def up_z(array, by):
    pairs = [(z * NY + y, (z + by) * NY + y) for z in range(NZ - by) for y in range(NY)]
    return lax.ppermute(array, "tm", pairs)


def qkv_kernel(place, first_ref, second_ref, gain_ref, w_ref, *refs):
    out_ref = refs[-1]
    rows = jnp.concatenate([first_ref[...], second_ref[...]], axis=0)
    blocks = [(kind, h) for kind in range(3) for h in range(LOCAL_HEADS)]
    for n in range(0, len(blocks), 2):
        pair = blocks[n : n + 2]
        weight = [w_ref[kind, :, h * HEAD : (h + 1) * HEAD] for kind, h in pair]
        weight = jnp.concatenate(weight, axis=1) if len(pair) > 1 else weight[0]
        proj = jnp.dot(rows, weight, preferred_element_type=F32)
        for m, (kind, h) in enumerate(pair):
            part = proj[:, m * HEAD : (m + 1) * HEAD]
            if kind < 2:
                inverse = lax.rsqrt(jnp.mean(part * part, axis=-1, keepdims=True) + eps_norm)
                part = part * inverse * gain_ref[kind : kind + 1, :]
            out_ref[place, kind, :, h * HEAD : (h + 1) * HEAD] = part.astype(BF)


def qkv_tile(first, second, place, gain, weight, held):
    earlier = [] if held is None else [held]
    return pl.pallas_call(
        functools.partial(qkv_kernel, place),
        in_specs=[VMEM] * (4 + len(earlier)),
        out_specs=VMEM,
        out_shape=jax.ShapeDtypeStruct((NX, 3, BLOCK, WIDTH), BF),
        input_output_aliases={4: 0} if earlier else {},
        compiler_params=pltpu.CompilerParams(vmem_limit_bytes=12 << 20),
        cost_estimate=pl.CostEstimate(flops=1, bytes_accessed=1, transcendentals=0),
        name="qkv_tile",
    )(first, second, gain, weight, *earlier)


def attend_kernel(place, list_ref, held_ref, out_ref):
    x = lax.axis_index("seq") // 2
    factor = 1.0 / math.sqrt(HEAD)
    ones = jnp.ones((BLOCK, HEAD), BF)
    for h in range(LOCAL_HEADS):
        cols = slice(h * HEAD, (h + 1) * HEAD)
        tiles = [(list_ref[h, (x + place) % NX, n] - x) % NX for n in range(3)]
        query = held_ref[place, 0, :, cols]
        scores = [
            lax.dot_general(
                query, held_ref[t, 1, :, cols], (((1,), (1,)), ((), ())), preferred_element_type=F32
            )
            for t in tiles
        ]
        top = functools.reduce(jnp.maximum, [jnp.max(s, axis=-1, keepdims=True) for s in scores])
        total = jnp.zeros((BLOCK, 2 * HEAD), F32)
        for s, t in zip(scores, tiles):
            probs = jnp.exp((s - top) * factor).astype(BF)
            values = jnp.concatenate([held_ref[t, 2, :, cols], ones], axis=1)
            total += jnp.dot(probs, values, preferred_element_type=F32)
        out_ref[:, cols] = (total[:, :HEAD] / total[:, HEAD:]).astype(BF)


def attend_tile(block_list, place, held):
    return pl.pallas_call(
        functools.partial(attend_kernel, place),
        in_specs=[SMEM, VMEM],
        out_specs=VMEM,
        out_shape=jax.ShapeDtypeStruct((BLOCK, WIDTH), BF),
        compiler_params=pltpu.CompilerParams(vmem_limit_bytes=12 << 20),
        cost_estimate=pl.CostEstimate(flops=1, bytes_accessed=1, transcendentals=0),
        name="attend_tile",
    )(block_list, held)


def out_kernel(half, p0, p1, p2, p3, w_ref, out_ref, rows):
    x = lax.axis_index("seq") // 2

    @pl.when(pl.program_id(0) == 0)
    def _():
        for d in range(NX):
            part = [p[d, half] for p in (p0, p1, p2, p3)]
            rows[:, d * WIDTH : (d + 1) * WIDTH] = jnp.concatenate(part, axis=0)

    weight = [w_ref[z, 0, (x - d) % NX] for d in range(NX) for z in range(NZ)]
    weight = jnp.concatenate(weight, axis=0)
    proj = jnp.dot(rows[...], weight, preferred_element_type=F32)
    out_ref[0] = proj.astype(out_ref.dtype)


def out_half(pieces, half, gathered, dtype):
    piece = pl.BlockSpec((NX, 2, SUB, WIDTH), lambda n: (0, 0, 0, 0))
    return pl.pallas_call(
        functools.partial(out_kernel, half),
        grid=(NY,),
        in_specs=[piece] * 4
        + [pl.BlockSpec((NZ, 1, NX, DEEP, COLS), lambda n: (0, n, 0, 0, 0))],
        out_specs=pl.BlockSpec((1, ROWS, COLS), lambda n: (n, 0, 0)),
        out_shape=jax.ShapeDtypeStruct((NY, ROWS, COLS), dtype),
        scratch_shapes=[pltpu.VMEM((ROWS, NX * WIDTH), BF)],
        compiler_params=pltpu.CompilerParams(vmem_limit_bytes=40 << 20),
        cost_estimate=pl.CostEstimate(flops=1, bytes_accessed=1, transcendentals=0),
        name="out_half",
    )(*pieces, gathered)


def row_kernel(own_ref, other_ref, gate_ref, part_ref, total_ref, held):
    y = lax.axis_index("tm") % NY
    for d in range(NY):
        term = own_ref[0, d] + other_ref[0, d].astype(F32)
        at = (y - d) % NY
        held[at] = gate_ref[pl.ds(at, 1), :] * term
    held[1] = held[0] + held[1]
    held[2] = held[1] + held[2]
    held[3] = held[2] + held[3]
    total_ref[0] = held[3].astype(BF)
    for d in range(NY):
        part_ref[d, 0] = held[(y - d) % NY]


def row_prefix(own, other, gates):
    block = pl.BlockSpec((1, NY, SUB, COLS), lambda n: (n, 0, 0, 0))
    return pl.pallas_call(
        row_kernel,
        grid=(NY,),
        in_specs=[block, block, pl.BlockSpec((NY, COLS), lambda n: (0, n))],
        out_specs=[
            pl.BlockSpec((NY, 1, SUB, COLS), lambda n: (0, n, 0, 0)),
            pl.BlockSpec((1, SUB, COLS), lambda n: (n, 0, 0)),
        ],
        out_shape=[
            jax.ShapeDtypeStruct((NY, NY, SUB, COLS), F32),
            jax.ShapeDtypeStruct((NY, SUB, COLS), BF),
        ],
        scratch_shapes=[pltpu.VMEM((NY, SUB, COLS), F32)],
        compiler_params=pltpu.CompilerParams(vmem_limit_bytes=32 << 20),
        cost_estimate=pl.CostEstimate(flops=1, bytes_accessed=1, transcendentals=0),
        name="row_prefix",
    )(own.reshape(NY, NY, SUB, COLS), other.reshape(NY, NY, SUB, COLS), gates)


def final_kernel(lat_ref, *refs):
    pieces, firsts, out_ref = refs[:4], refs[4:8], refs[8]
    step = lax.axis_index("tm")
    y = step % NY
    for d in range(NY):
        at = (y + d) % NY
        first = jnp.where(step == 0, lat_ref[at], firsts[d][...])
        out_ref[at] = first + pieces[d][0].astype(F32)


def final_sum(latents, pieces, firsts):
    piece = pl.BlockSpec((1, SUB, COLS), lambda n: (n, 0, 0))
    first = pl.BlockSpec((SUB, COLS), lambda n: (0, n))
    block = pl.BlockSpec((NY, SUB, COLS), lambda n: (0, 0, n))
    return pl.pallas_call(
        final_kernel,
        grid=(NY,),
        in_specs=[block] + [piece] * 4 + [first] * 4,
        out_specs=block,
        out_shape=jax.ShapeDtypeStruct((NY, SUB, D), F32),
        compiler_params=pltpu.CompilerParams(vmem_limit_bytes=32 << 20),
        cost_estimate=pl.CostEstimate(flops=1, bytes_accessed=1, transcendentals=0),
        name="final_sum",
    )(latents.reshape(NY, SUB, D), *pieces, *firsts)


def barrier(*arrays):
    return lax.optimization_barrier(arrays)


def per_device(latents, timesteps, mod_weight, qkv_weight, qk_gain, out_weight, block_list):
    step = lax.axis_index("tm")
    z, y = step // NY, step % NY

    piece = lax.dynamic_slice(out_weight, (z * DEEP, y * COLS), (DEEP, COLS))
    groups = [[i * 2 + c for i in range(NZ * NY * NX)] for c in range(2)]
    gathered = lax.all_gather(piece, ("tm", "seq"), axis_index_groups=groups)
    gathered = gathered.reshape(NZ, NY, NX, DEEP, COLS)

    modulated, gates = modulate(latents, timesteps, mod_weight)

    twin = swap_core(modulated)
    before = shift_x(modulated, 1)
    after = shift_x(modulated, -1)

    twin, current = barrier(twin, latents[0])
    half = current.astype(jnp.float16).reshape(NY, SUB, D)
    parts = [lax.ppermute(half[to], "tm", [(0, to)]) for to in range(1, NY)]
    held = qkv_tile(modulated, twin, 0, qk_gain, qkv_weight, None)

    before, after, held, parts, half = barrier(before, after, held, parts, half)
    far = opposite_x(before, after)
    quarter = half[0]
    for to in range(1, NY):
        quarter = jnp.where(y == to, parts[to - 1], quarter)
    parts = [
        lax.ppermute(quarter, "tm", [(n, to * NY + n) for n in range(NY)]) for to in range(1, NZ)
    ]
    held = qkv_tile(after, swap_core(after), 1, qk_gain, qkv_weight, held)
    held = qkv_tile(before, swap_core(before), 3, qk_gain, qkv_weight, held)
    far, held, parts, quarter = barrier(far, held, parts, quarter)
    for to in range(1, NZ):
        quarter = jnp.where(z == to, parts[to - 1], quarter)
    firsts = [shift_y(quarter, -d) if d else quarter for d in range(NY)]
    held = qkv_tile(far, swap_core(far), 2, qk_gain, qkv_weight, held)

    arrived = [None] * NX
    for d in (2, 1, 3, 0):
        attended = attend_tile(block_list, d, held)
        if d == 0:
            attended, firsts = barrier(attended, firsts)
        arrived[d] = shift_x(attended, d) if d else attended
    rows = jnp.stack(arrived).reshape(NX, 2, NY, SUB, WIDTH)

    pieces = []
    for d in range(NY):
        send = lax.dynamic_index_in_dim(rows, (y + d) % NY, 2, keepdims=False)
        pieces.append(shift_y(send, d) if d else send)

    other = swap_core(out_half(pieces, 1, gathered, BF))
    own = out_half(pieces, 0, gathered, F32)
    parts, total = row_prefix(own, other, gates)
    base = sum(up_z(total, by).astype(F32) for by in range(1, NZ))

    back = []
    for d in range(NY):
        send = (parts[d] + base).astype(BF)
        back.append(shift_y(send, -d) if d else send)
    firsts = [part.astype(F32) for part in firsts]
    return final_sum(latents, back, firsts).reshape(1, ROWS, D)


def solution(mesh):
    return jax.shard_map(
        per_device,
        mesh=mesh,
        in_specs=(
            P("tm", "seq", None),
            P(),
            P(),
            P(None, None, "seq"),
            P(),
            P("seq", None),
            P("seq", None, None),
        ),
        out_specs=P("tm", "seq", None),
        check_vma=False,
    )
```

```python
import functools
import math

import jax
import jax.numpy as jnp
from jax import lax
from jax.experimental import pallas as pl
from jax.experimental.pallas import tpu as pltpu
from jax.sharding import PartitionSpec as P

D = 3072
BLOCK = 384
HEAD = 128
LOCAL_HEADS = 3
WIDTH = LOCAL_HEADS * HEAD
NX = 4
NY = 4
NZ = 4
ROWS = 192
SUB = 48
COLS = D // NY
DEEP = WIDTH // NZ
eps_norm = 1e-06

BF = jnp.bfloat16
F32 = jnp.float32
VMEM = pl.BlockSpec(memory_space=pltpu.VMEM)
SMEM = pl.BlockSpec(memory_space=pltpu.SMEM)


def modulate_kernel(stamps_ref, freq_ref, w_hbm, lat_hbm, out_ref, gate_ref, w, lat, held, w_sems, lat_sems):
    step = lax.axis_index("tm")
    row, y = step // NY, step % NY
    lat_copies = [
        pltpu.make_async_copy(lat_hbm.at[0, part], lat.at[part], lat_sems.at[n])
        for n, part in enumerate(pl.ds(n * SUB, SUB) for n in range(4))
    ]
    w_copies = [
        pltpu.make_async_copy(w_hbm.at[:, part], w.at[:, part], w_sems.at[n])
        for n, part in enumerate(pl.ds(n * D, D) for n in range(3))
    ]
    for copy in lat_copies + w_copies:
        copy.start()

    lane = lax.broadcasted_iota(jnp.int32, (8, HEAD), 0)
    stamps = jnp.zeros((8, HEAD), F32)
    for n in range(NY):
        stamps = jnp.where(lane == n, stamps_ref[row * NY + n].astype(F32), stamps)
    angles = stamps * freq_ref[...]
    emb = jnp.concatenate([jnp.cos(angles), jnp.sin(angles)], axis=1).astype(BF)

    for n in range(4):
        lat_copies[n].wait()
        part = slice(n * SUB, (n + 1) * SUB)
        current = lat[part, :]
        centred = current - jnp.mean(current, axis=-1, keepdims=True)
        var = jnp.mean(centred * centred, axis=-1, keepdims=True)
        lat[part, :] = centred * lax.rsqrt(var + eps_norm)

    def project(n):
        w_copies[n].wait()
        held[:, n * D : (n + 1) * D] = jnp.dot(
            emb, w[:, n * D : (n + 1) * D], preferred_element_type=F32
        )

    project(0)
    project(1)
    shift = held[pl.ds(y, 1), :D]
    scale = held[pl.ds(y, 1), D : 2 * D]
    for n in range(4):
        part = slice(n * SUB, (n + 1) * SUB)
        out_ref[part, :] = (lat[part, :] * (1.0 + scale) + shift).astype(BF)
    project(2)
    for n in range(NY):
        delta = (stamps_ref[row * NY + n + 1] - stamps_ref[row * NY + n]).astype(F32) / 1000.0
        gate_ref[n : n + 1, :] = held[n : n + 1, 2 * D :] * delta


def modulate(latents, timesteps, mod_weight):
    half = mod_weight.shape[0] // 2
    freqs = jnp.exp(-jnp.log(10000.0) * jnp.arange(half, dtype=F32) / half)
    return pl.pallas_call(
        modulate_kernel,
        in_specs=[
            pl.BlockSpec(memory_space=pltpu.SMEM),
            VMEM,
            pl.BlockSpec(memory_space=pl.ANY),
            pl.BlockSpec(memory_space=pl.ANY),
        ],
        out_specs=[VMEM, VMEM],
        out_shape=[
            jax.ShapeDtypeStruct((ROWS, D), BF),
            jax.ShapeDtypeStruct((NY, D), F32),
        ],
        scratch_shapes=[
            pltpu.VMEM((2 * half, 3 * D), BF),
            pltpu.VMEM((ROWS, D), F32),
            pltpu.VMEM((8, 3 * D), F32),
            pltpu.SemaphoreType.DMA((3,)),
            pltpu.SemaphoreType.DMA((4,)),
        ],
        compiler_params=pltpu.CompilerParams(vmem_limit_bytes=58 << 20),
        cost_estimate=pl.CostEstimate(
            flops=10 * ROWS * D, bytes_accessed=9_000_000, transcendentals=ROWS
        ),
        name="modulate",
    )(timesteps, freqs[None], mod_weight, latents)


def shift_x(array, by):
    return lax.ppermute(array, "seq", [(i, (i + 2 * by) % 8) for i in range(8)])


def swap_core(array):
    return lax.ppermute(array, "seq", [(i, i ^ 1) for i in range(8)])


def shift_y(array, by):
    pairs = [(z * NY + y, z * NY + (y + by) % NY) for z in range(NZ) for y in range(NY)]
    return lax.ppermute(array, "tm", pairs)


def opposite_x(forward, backward):
    core = lax.axis_index("seq") % 2
    send = jnp.where(core == 0, forward, backward)
    return lax.ppermute(send, "seq", [(i, (i + 2 - 4 * (i % 2)) % 8) for i in range(8)])


def up_z(array, by):
    pairs = [(z * NY + y, (z + by) * NY + y) for z in range(NZ - by) for y in range(NY)]
    return lax.ppermute(array, "tm", pairs)


def qkv_kernel(places, *refs):
    parts, (gain_ref, w_ref), out_ref = refs[: 2 * len(places)], refs[2 * len(places) :][:2], refs[-1]
    rows = jnp.concatenate([part[...] for part in parts], axis=0)
    blocks = [(kind, h) for kind in range(3) for h in range(LOCAL_HEADS)]
    for n in range(0, len(blocks), 2):
        pair = blocks[n : n + 2]
        weight = [w_ref[kind, :, h * HEAD : (h + 1) * HEAD] for kind, h in pair]
        weight = jnp.concatenate(weight, axis=1) if len(pair) > 1 else weight[0]
        proj = jnp.dot(rows, weight, preferred_element_type=F32)
        for m, (kind, h) in enumerate(pair):
            part = proj[:, m * HEAD : (m + 1) * HEAD]
            if kind < 2:
                inverse = lax.rsqrt(jnp.mean(part * part, axis=-1, keepdims=True) + eps_norm)
                part = part * inverse * gain_ref[kind : kind + 1, :]
            part = part.astype(BF)
            for t, place in enumerate(places):
                out_ref[place, kind, :, h * HEAD : (h + 1) * HEAD] = part[t * BLOCK : (t + 1) * BLOCK]


def qkv_tiles(parts, places, gain, weight, held):
    earlier = [] if held is None else [held]
    return pl.pallas_call(
        functools.partial(qkv_kernel, places),
        in_specs=[VMEM] * (len(parts) + 2 + len(earlier)),
        out_specs=VMEM,
        out_shape=jax.ShapeDtypeStruct((NX, 3, BLOCK, WIDTH), BF),
        input_output_aliases={len(parts) + 2: 0} if earlier else {},
        compiler_params=pltpu.CompilerParams(vmem_limit_bytes=16 << 20),
        cost_estimate=pl.CostEstimate(
            flops=2 * len(places) * BLOCK * D * 3 * WIDTH, bytes_accessed=10_000_000, transcendentals=0
        ),
        name="qkv_tiles",
    )(*parts, gain, weight, *earlier)


def attend_kernel(place, list_ref, held_ref, out_ref):
    x = lax.axis_index("seq") // 2
    factor = 1.0 / math.sqrt(HEAD)
    ones = jnp.ones((BLOCK, HEAD), BF)
    for h in range(LOCAL_HEADS):
        cols = slice(h * HEAD, (h + 1) * HEAD)
        tiles = [(list_ref[h, (x + place) % NX, n] - x) % NX for n in range(3)]
        query = held_ref[place, 0, :, cols]
        scores = [
            lax.dot_general(
                query, held_ref[t, 1, :, cols], (((1,), (1,)), ((), ())), preferred_element_type=F32
            )
            for t in tiles
        ]
        top = functools.reduce(jnp.maximum, [jnp.max(s, axis=-1, keepdims=True) for s in scores])
        total = jnp.zeros((BLOCK, 2 * HEAD), F32)
        for s, t in zip(scores, tiles):
            probs = jnp.exp((s - top) * factor).astype(BF)
            values = jnp.concatenate([held_ref[t, 2, :, cols], ones], axis=1)
            total += jnp.dot(probs, values, preferred_element_type=F32)
        out_ref[:, cols] = (total[:, :HEAD] / total[:, HEAD:]).astype(BF)


def attend_tile(block_list, place, held):
    return pl.pallas_call(
        functools.partial(attend_kernel, place),
        in_specs=[SMEM, VMEM],
        out_specs=VMEM,
        out_shape=jax.ShapeDtypeStruct((BLOCK, WIDTH), BF),
        compiler_params=pltpu.CompilerParams(vmem_limit_bytes=12 << 20),
        cost_estimate=pl.CostEstimate(
            flops=4 * 3 * BLOCK * 3 * BLOCK * HEAD, bytes_accessed=4_000_000, transcendentals=0
        ),
        name="attend_tile",
    )(block_list, held)


def pack_kernel(a0, a1, a2, a3, *outs):
    y = lax.axis_index("tm") % NY
    for d, out_ref in enumerate(outs):
        sub = (y + d) % NY
        for n, a in enumerate((a0, a1, a2, a3)):
            for half in range(2):
                at = pl.multiple_of(half * ROWS + sub * SUB, 16)
                out_ref[n, half] = a[pl.ds(at, SUB), :]


def pack(arrived):
    return pl.pallas_call(
        pack_kernel,
        in_specs=[VMEM] * NX,
        out_specs=[VMEM] * NY,
        out_shape=[jax.ShapeDtypeStruct((NX, 2, SUB, WIDTH), BF)] * NY,
        compiler_params=pltpu.CompilerParams(vmem_limit_bytes=12 << 20),
        cost_estimate=pl.CostEstimate(flops=1, bytes_accessed=40_000_000, transcendentals=0),
        name="pack",
    )(*arrived)


def out_kernel(p0, p1, p2, p3, own_ref, w_ref, gate_ref, mine_ref, other_ref, rows):
    y = lax.axis_index("tm") % NY
    for half in range(2):
        for d in range(NX):
            part = [p[d, half] for p in (p0, p1, p2, p3)]
            at = slice(half * ROWS, (half + 1) * ROWS)
            rows[at, d * WIDTH : (d + 1) * WIDTH] = jnp.concatenate(part, axis=0)
    for n in range(NY):
        cols = slice(n * COLS, (n + 1) * COLS)
        block = [own_ref[:, cols]]
        block += [w_ref[z, n, d] for d in range(NX - 1) for z in range(NZ)]
        block = jnp.concatenate(block, axis=0)
        proj = jnp.dot(rows[...], block, preferred_element_type=F32)
        for d in range(NY):
            gate = gate_ref[pl.ds((y - d) % NY, 1), cols]
            mine_ref[n, d] = (proj[d * SUB : (d + 1) * SUB] * gate).astype(BF)
            other_ref[n, d] = (proj[ROWS + d * SUB : ROWS + (d + 1) * SUB] * gate).astype(BF)


def out_project(pieces, own, gathered, gates):
    return pl.pallas_call(
        out_kernel,
        in_specs=[VMEM] * 7,
        out_specs=[VMEM] * 2,
        out_shape=[jax.ShapeDtypeStruct((NY, NY, SUB, COLS), BF)] * 2,
        scratch_shapes=[pltpu.VMEM((2 * ROWS, NX * WIDTH), BF)],
        compiler_params=pltpu.CompilerParams(vmem_limit_bytes=12 << 20),
        cost_estimate=pl.CostEstimate(
            flops=4 * ROWS * NX * WIDTH * D, bytes_accessed=12_000_000, transcendentals=0
        ),
        name="out_project",
    )(*pieces, own, gathered, gates)


def row_kernel(part, own_ref, other_ref, part_ref, total_ref, held):
    y = lax.axis_index("tm") % NY
    for n in range(2):
        for d in range(NY):
            at = 2 * part + n
            held[(y - d) % NY] = own_ref[at, d].astype(F32) + other_ref[at, d].astype(F32)
        held[1] = held[0] + held[1]
        held[2] = held[1] + held[2]
        held[3] = held[2] + held[3]
        total_ref[n] = held[3].astype(BF)
        for d in range(NY):
            part_ref[d, n] = held[(y - d) % NY]


def row_prefix(part, own, other):
    return pl.pallas_call(
        functools.partial(row_kernel, part),
        in_specs=[VMEM] * 2,
        out_specs=[VMEM] * 2,
        out_shape=[
            jax.ShapeDtypeStruct((NY, 2, SUB, COLS), F32),
            jax.ShapeDtypeStruct((2, SUB, COLS), BF),
        ],
        scratch_shapes=[pltpu.VMEM((NY, SUB, COLS), F32)],
        compiler_params=pltpu.CompilerParams(vmem_limit_bytes=12 << 20),
        cost_estimate=pl.CostEstimate(flops=1, bytes_accessed=2_000_000, transcendentals=0),
        name="row_prefix",
    )(own, other)


def final_kernel(lat_ref, *refs):
    pieces, firsts, out_ref = refs[:4], refs[4:8], refs[-1]
    step = lax.axis_index("tm")
    y = step % NY
    for d in range(NY):
        at = (y + d) % NY
        first = jnp.where(step == 0, lat_ref[at], firsts[d][...])
        out_ref[at] = first + pieces[d][0].astype(F32)


def final_sum(part, latents, pieces, firsts, earlier):
    piece = pl.BlockSpec((1, SUB, COLS), lambda n: (n, 0, 0))
    first = pl.BlockSpec((SUB, COLS), lambda n: (0, 2 * part + n))
    block = pl.BlockSpec((NY, SUB, COLS), lambda n: (0, 0, 2 * part + n))
    more = [] if earlier is None else [earlier]
    return pl.pallas_call(
        final_kernel,
        grid=(2,),
        in_specs=[block] + [piece] * 4 + [first] * 4 + [pl.BlockSpec(memory_space=pl.ANY)] * len(more),
        out_specs=block,
        out_shape=jax.ShapeDtypeStruct((NY, SUB, D), F32),
        input_output_aliases={9: 0} if more else {},
        compiler_params=pltpu.CompilerParams(vmem_limit_bytes=12 << 20),
        cost_estimate=pl.CostEstimate(flops=1, bytes_accessed=1, transcendentals=0),
        name="final_sum",
    )(latents.reshape(NY, SUB, D), *pieces, *firsts, *more)


def barrier(*arrays):
    return lax.optimization_barrier(arrays)


def per_device(latents, timesteps, mod_weight, qkv_weight, qk_gain, out_weight, block_list):
    step = lax.axis_index("tm")
    z, y = step // NY, step % NY

    piece = lax.dynamic_slice(out_weight, (z * DEEP, y * COLS), (DEEP, COLS))
    pieces = [shift_x(piece, d) for d in range(1, NX)]
    modulated, gates = modulate(latents, timesteps, mod_weight)
    modulated, pieces = barrier(modulated, pieces)
    gathered = lax.all_gather(jnp.stack(pieces), "tm").reshape(NZ, NY, NX - 1, DEEP, COLS)

    twin = swap_core(modulated)
    before = shift_x(modulated, 1)
    after = shift_x(modulated, -1)

    twin, current, weight = barrier(twin, latents[0], qkv_weight)
    half = current.astype(jnp.float16).reshape(NY, SUB, D)
    parts = [lax.ppermute(half[to], "tm", [(0, to)]) for to in range(1, NY)]
    held = qkv_tiles([modulated, twin], (0,), qk_gain, weight, None)

    before, after, held, parts, half = barrier(before, after, held, parts, half)
    far = opposite_x(before, after)
    quarter = half[0]
    for to in range(1, NY):
        quarter = jnp.where(y == to, parts[to - 1], quarter)
    near = [after, swap_core(after), before, swap_core(before)]
    held = qkv_tiles(near, (1, 3), qk_gain, weight, held)
    far, held, quarter = barrier(far, held, quarter)
    held = qkv_tiles([far, swap_core(far)], (2,), qk_gain, weight, held)

    arrived = [None] * NX
    for d in (2, 1, 3, 0):
        if d == 0:
            held, arrived[2] = barrier(held, arrived[2])
        attended = attend_tile(block_list, d, held)
        arrived[d] = shift_x(attended, d) if d else attended

    arrived, gathered, quarter, own_weight = barrier(arrived, gathered, quarter, out_weight)
    pieces = pack(arrived)
    pieces = [shift_y(send, d) if d else send for d, send in enumerate(pieces)]
    got = lax.ppermute(quarter, "tm", [(n, 2 * NY + n) for n in range(NY)])
    quarter = jnp.where(z == 2, got, quarter)
    pieces, quarter = barrier(pieces, quarter)
    got = lax.ppermute(
        quarter, "tm", [(at * NY + n, (at + 1) * NY + n) for n in range(NY) for at in (0, 2)]
    )
    own, other = out_project(pieces, own_weight, gathered, gates)

    own, other, got, quarter = barrier(own, other, got, quarter)
    other = swap_core(other)
    quarter = jnp.where(z % 2 == 1, got, quarter)
    firsts = [shift_y(quarter, -d) if d else quarter for d in range(NY)]

    result = None
    for part in range(2):
        parts, total = row_prefix(part, own, other)
        base = sum(up_z(total, by).astype(F32) for by in range(1, NZ))
        back = []
        for d in range(NY):
            send = (parts[d] + base).astype(BF)
            back.append(shift_y(send, -d) if d else send)
        if part == 0:
            firsts = [first.astype(F32) for first in firsts]
        result = final_sum(part, latents, back, firsts, result)
    return result.reshape(1, ROWS, D)


def solution(mesh):
    return jax.shard_map(
        per_device,
        mesh=mesh,
        in_specs=(
            P("tm", "seq", None),
            P(),
            P(),
            P(None, None, "seq"),
            P(),
            P("seq", None),
            P("seq", None, None),
        ),
        out_specs=P("tm", "seq", None),
        check_vma=False,
    )
```

```python
import functools
import math

import jax
import jax.numpy as jnp
from jax import lax
from jax.experimental import pallas as pl
from jax.experimental.pallas import tpu as pltpu
from jax.sharding import PartitionSpec as P

D = 3072
BLOCK = 384
HEAD = 128
LOCAL_HEADS = 3
WIDTH = LOCAL_HEADS * HEAD
NX = 4
NY = 4
NZ = 4
ROWS = 192
SUB = 48
COLS = D // NY
DEEP = WIDTH // NZ
PARTS = 2
PER = NY // PARTS
eps_norm = 1e-06

BF = jnp.bfloat16
F32 = jnp.float32
VMEM = pl.BlockSpec(memory_space=pltpu.VMEM)
SMEM = pl.BlockSpec(memory_space=pltpu.SMEM)


def row_embedding(stamps_ref, row):
    lane = lax.broadcasted_iota(jnp.int32, (8, HEAD), 0)
    stamps = jnp.zeros((8, HEAD), F32)
    for n in range(NY):
        stamps = jnp.where(lane == n, stamps_ref[row * NY + n].astype(F32), stamps)
    place = lax.broadcasted_iota(jnp.int32, (8, HEAD), 1).astype(F32)
    angles = stamps * jnp.exp(-math.log(10000.0) * place / HEAD)
    return jnp.concatenate([jnp.cos(angles), jnp.sin(angles)], axis=1).astype(BF)


def modulate_kernel(stamps_ref, w_hbm, lat_hbm, out_ref, w, lat, held, w_sems, lat_sems):
    step = lax.axis_index("tm")
    row, y = step // NY, step % NY
    lat_copies = [
        pltpu.make_async_copy(
            lat_hbm.at[0, pl.ds(n * SUB, SUB)], lat.at[pl.ds(n * SUB, SUB)], lat_sems.at[n]
        )
        for n in range(4)
    ]
    w_copies = [
        pltpu.make_async_copy(w_hbm.at[:, pl.ds(n * D, D)], w.at[:, pl.ds(n * D, D)], w_sems.at[n])
        for n in range(2)
    ]
    for copy in lat_copies + w_copies:
        copy.start()
    emb = row_embedding(stamps_ref, row)
    for n in range(4):
        lat_copies[n].wait()
        part = slice(n * SUB, (n + 1) * SUB)
        current = lat[part, :]
        centred = current - jnp.mean(current, axis=-1, keepdims=True)
        var = jnp.mean(centred * centred, axis=-1, keepdims=True)
        lat[part, :] = centred * lax.rsqrt(var + eps_norm)
    for n in range(2):
        w_copies[n].wait()
        cols = slice(n * D, (n + 1) * D)
        held[:, cols] = jnp.dot(emb, w[:, cols], preferred_element_type=F32)
    shift = held[pl.ds(y, 1), :D]
    scale = held[pl.ds(y, 1), D:]
    for n in range(4):
        part = slice(n * SUB, (n + 1) * SUB)
        out_ref[part, :] = (lat[part, :] * (1.0 + scale) + shift).astype(BF)


def modulate(latents, timesteps, mod_weight):
    depth = mod_weight.shape[0]
    return pl.pallas_call(
        modulate_kernel,
        in_specs=[SMEM] + [pl.BlockSpec(memory_space=pl.ANY)] * 2,
        out_specs=VMEM,
        out_shape=jax.ShapeDtypeStruct((ROWS, D), BF),
        scratch_shapes=[
            pltpu.VMEM((depth, 2 * D), BF),
            pltpu.VMEM((ROWS, D), F32),
            pltpu.VMEM((8, 2 * D), F32),
            pltpu.SemaphoreType.DMA((2,)),
            pltpu.SemaphoreType.DMA((4,)),
        ],
        compiler_params=pltpu.CompilerParams(vmem_limit_bytes=58 << 20),
        cost_estimate=pl.CostEstimate(
            flops=10 * ROWS * D, bytes_accessed=9_000_000, transcendentals=ROWS
        ),
        name="modulate",
    )(timesteps, mod_weight, latents)


def gate_kernel(stamps_ref, w_ref, gate_ref):
    row = lax.axis_index("tm") // NY
    gates = jnp.dot(row_embedding(stamps_ref, row), w_ref[...], preferred_element_type=F32)
    for n in range(NY):
        delta = (stamps_ref[row * NY + n + 1] - stamps_ref[row * NY + n]).astype(F32) / 1000.0
        gate_ref[n : n + 1, :] = gates[n : n + 1, :] * delta


def row_gates(timesteps, mod_weight):
    return pl.pallas_call(
        gate_kernel,
        grid=(1,),
        in_specs=[SMEM, pl.BlockSpec((mod_weight.shape[0], D), lambda n: (0, 2))],
        out_specs=pl.BlockSpec((NY, D), lambda n: (0, 0)),
        out_shape=jax.ShapeDtypeStruct((NY, D), F32),
        compiler_params=pltpu.CompilerParams(vmem_limit_bytes=10 << 20),
        cost_estimate=pl.CostEstimate(flops=1, bytes_accessed=2_000_000, transcendentals=0),
        name="row_gates",
    )(timesteps, mod_weight)


def shift_x(array, by):
    return lax.ppermute(array, "seq", [(i, (i + 2 * by) % 8) for i in range(8)])


def swap_core(array):
    return lax.ppermute(array, "seq", [(i, i ^ 1) for i in range(8)])


def shift_y(array, by):
    pairs = [(z * NY + y, z * NY + (y + by) % NY) for z in range(NZ) for y in range(NY)]
    return lax.ppermute(array, "tm", pairs)


def opposite_x(first_core, forward, backward):
    send = jnp.where(first_core, forward, backward)
    return lax.ppermute(send, "seq", [(i, (i + 2 - 4 * (i % 2)) % 8) for i in range(8)])


def shift_z(array, by):
    pairs = [(z * NY + y, (z + by) % NZ * NY + y) for z in range(NZ) for y in range(NY)]
    return lax.ppermute(array, "tm", pairs)


def load_kernel(*refs):
    count = (len(refs) - 1) // 2
    sems = refs[-1]
    copies = [pltpu.make_async_copy(refs[n], refs[count + n], sems.at[n]) for n in range(count)]
    for copy in copies:
        copy.start()
    for copy in copies:
        copy.wait()


def load(*arrays):
    return pl.pallas_call(
        load_kernel,
        in_specs=[pl.BlockSpec(memory_space=pltpu.HBM)] * len(arrays),
        out_specs=[VMEM] * len(arrays),
        out_shape=[jax.ShapeDtypeStruct(a.shape, a.dtype) for a in arrays],
        scratch_shapes=[pltpu.SemaphoreType.DMA((len(arrays),))],
        compiler_params=pltpu.CompilerParams(vmem_limit_bytes=11 << 20),
        cost_estimate=pl.CostEstimate(
            flops=1, bytes_accessed=2 * sum(a.size * 2 for a in arrays), transcendentals=0
        ),
        name="load",
    )(*arrays)


def qkv_kernel(places, *refs):
    parts, (gain_ref, w_ref), out_ref = refs[: len(places)], refs[len(places) :][:2], refs[-1]
    rows = jnp.concatenate([part[...] for part in parts], axis=0) if len(parts) > 1 else parts[0][...]
    blocks = [(kind, h) for kind in range(3) for h in range(LOCAL_HEADS)]
    for n in range(0, len(blocks), 2):
        pair = blocks[n : n + 2]
        weight = [w_ref[kind, :, h * HEAD : (h + 1) * HEAD] for kind, h in pair]
        weight = jnp.concatenate(weight, axis=1) if len(pair) > 1 else weight[0]
        proj = jnp.dot(rows, weight, preferred_element_type=F32)
        for m, (kind, h) in enumerate(pair):
            part = proj[:, m * HEAD : (m + 1) * HEAD]
            if kind < 2:
                inverse = lax.rsqrt(jnp.mean(part * part, axis=-1, keepdims=True) + eps_norm)
                part = part * inverse * gain_ref[kind : kind + 1, :]
            part = part.astype(BF)
            for t, (place, half) in enumerate(places):
                at = slice(half * ROWS, (half + 1) * ROWS)
                out_ref[place, kind, at, h * HEAD : (h + 1) * HEAD] = part[t * ROWS : (t + 1) * ROWS]


def qkv_tiles(parts, places, gain, weight, held):
    earlier = [] if held is None else [held]
    return pl.pallas_call(
        functools.partial(qkv_kernel, places),
        in_specs=[VMEM] * (len(parts) + 2 + len(earlier)),
        out_specs=VMEM,
        out_shape=jax.ShapeDtypeStruct((NX, 3, BLOCK, WIDTH), BF),
        input_output_aliases={len(parts) + 2: 0} if earlier else {},
        compiler_params=pltpu.CompilerParams(vmem_limit_bytes=11 << 20),
        cost_estimate=pl.CostEstimate(
            flops=2 * len(places) * ROWS * D * 3 * WIDTH, bytes_accessed=10_000_000, transcendentals=0
        ),
        name="qkv_tiles",
    )(*parts, gain, weight, *earlier)


def attend_kernel(place, list_ref, held_ref, out_ref):
    x = lax.axis_index("seq") // 2
    factor = 1.0 / math.sqrt(HEAD)
    ones = jnp.ones((BLOCK, HEAD), BF)
    for h in range(LOCAL_HEADS):
        cols = slice(h * HEAD, (h + 1) * HEAD)
        tiles = [(list_ref[h, (x + place) % NX, n] - x) % NX for n in range(3)]
        query = held_ref[place, 0, :, cols]
        scores = [
            lax.dot_general(
                query, held_ref[t, 1, :, cols], (((1,), (1,)), ((), ())), preferred_element_type=F32
            )
            for t in tiles
        ]
        top = functools.reduce(jnp.maximum, [jnp.max(s, axis=-1, keepdims=True) for s in scores])
        total = jnp.zeros((BLOCK, 2 * HEAD), F32)
        for s, t in zip(scores, tiles):
            probs = jnp.exp((s - top) * factor).astype(BF)
            values = jnp.concatenate([held_ref[t, 2, :, cols], ones], axis=1)
            total += jnp.dot(probs, values, preferred_element_type=F32)
        out_ref[:, cols] = (total[:, :HEAD] / total[:, HEAD:]).astype(BF)


def attend_tile(block_list, place, held):
    return pl.pallas_call(
        functools.partial(attend_kernel, place),
        in_specs=[SMEM, VMEM],
        out_specs=VMEM,
        out_shape=jax.ShapeDtypeStruct((BLOCK, WIDTH), BF),
        compiler_params=pltpu.CompilerParams(vmem_limit_bytes=12 << 20),
        cost_estimate=pl.CostEstimate(
            flops=4 * 3 * BLOCK * 3 * BLOCK * HEAD, bytes_accessed=4_000_000, transcendentals=0
        ),
        name="attend_tile",
    )(block_list, held)


def pack_kernel(a0, a1, a2, a3, o0, o1, o2, o3, sems):
    y = lax.axis_index("tm") % NY
    copies = []
    for d, out_ref in enumerate((o0, o1, o2, o3)):
        sub = (y + d) % NY
        for n, a in enumerate((a0, a1, a2, a3)):
            for half in range(2):
                at = pl.multiple_of(half * ROWS + sub * SUB, 16)
                copies.append(
                    pltpu.make_async_copy(
                        a.at[pl.ds(at, SUB)], out_ref.at[n, half], sems.at[d, n, half]
                    )
                )
    for copy in copies:
        copy.start()
    for copy in copies:
        copy.wait()


def pack(arrived):
    return pl.pallas_call(
        pack_kernel,
        in_specs=[pl.BlockSpec(memory_space=pl.ANY)] * NX,
        out_specs=[VMEM] * NY,
        out_shape=[jax.ShapeDtypeStruct((NX, 2, SUB, WIDTH), BF)] * NY,
        scratch_shapes=[pltpu.SemaphoreType.DMA((NY, NX, 2))],
        compiler_params=pltpu.CompilerParams(vmem_limit_bytes=4 << 20),
        cost_estimate=pl.CostEstimate(flops=1, bytes_accessed=40_000_000, transcendentals=0),
        name="pack",
    )(*arrived)


def out_kernel(p0, p1, p2, p3, own_ref, w_ref, gate_ref, mine_ref, other_ref, rows):
    y = lax.axis_index("tm") % NY
    for half in range(2):
        for d in range(NX):
            part = [p[d, half] for p in (p0, p1, p2, p3)]
            at = slice(half * ROWS, (half + 1) * ROWS)
            rows[at, d * WIDTH : (d + 1) * WIDTH] = jnp.concatenate(part, axis=0)
    for n in range(NY):
        cols = slice(n * COLS, (n + 1) * COLS)
        block = [own_ref[:, cols]]
        block += [w_ref[z, n, d] for d in range(NX - 1) for z in range(NZ)]
        block = jnp.concatenate(block, axis=0)
        proj = jnp.dot(rows[...], block, preferred_element_type=F32)
        for d in range(NY):
            gate = gate_ref[pl.ds((y - d) % NY, 1), cols]
            mine_ref[n, d] = (proj[d * SUB : (d + 1) * SUB] * gate).astype(BF)
            other_ref[n, d] = (proj[ROWS + d * SUB : ROWS + (d + 1) * SUB] * gate).astype(BF)


def out_project(pieces, own, gathered, gates):
    return pl.pallas_call(
        out_kernel,
        in_specs=[VMEM] * 7,
        out_specs=[VMEM] * 2,
        out_shape=[jax.ShapeDtypeStruct((NY, NY, SUB, COLS), BF)] * 2,
        scratch_shapes=[pltpu.VMEM((2 * ROWS, NX * WIDTH), BF)],
        compiler_params=pltpu.CompilerParams(vmem_limit_bytes=12 << 20),
        cost_estimate=pl.CostEstimate(
            flops=4 * ROWS * NX * WIDTH * D, bytes_accessed=12_000_000, transcendentals=0
        ),
        name="out_project",
    )(*pieces, own, gathered, gates)


def row_kernel(part, own_ref, other_ref, part_ref, total_ref, held):
    y = lax.axis_index("tm") % NY
    for n in range(PER):
        for d in range(NY):
            at = PER * part + n
            held[(y - d) % NY] = own_ref[at, d].astype(F32) + other_ref[at, d].astype(F32)
        held[1] = held[0] + held[1]
        held[2] = held[1] + held[2]
        held[3] = held[2] + held[3]
        total_ref[n] = held[3].astype(BF)
        for d in range(NY):
            part_ref[d, n] = held[(y - d) % NY]


def row_prefix(part, own, other):
    return pl.pallas_call(
        functools.partial(row_kernel, part),
        in_specs=[VMEM] * 2,
        out_specs=[VMEM] * 2,
        out_shape=[
            jax.ShapeDtypeStruct((NY, PER, SUB, COLS), F32),
            jax.ShapeDtypeStruct((PER, SUB, COLS), BF),
        ],
        scratch_shapes=[pltpu.VMEM((NY, SUB, COLS), F32)],
        compiler_params=pltpu.CompilerParams(vmem_limit_bytes=12 << 20),
        cost_estimate=pl.CostEstimate(flops=1, bytes_accessed=2_000_000, transcendentals=0),
        name="row_prefix",
    )(own, other)


def final_kernel(lat_ref, *refs):
    pieces, firsts, out_ref = refs[:4], refs[4:8], refs[-1]
    step = lax.axis_index("tm")
    y = step % NY
    for d in range(NY):
        at = (y + d) % NY
        first = jnp.where(step == 0, lat_ref[at], firsts[d][...])
        out_ref[at] = first + pieces[d][0].astype(F32)


def final_sum(part, latents, pieces, firsts, earlier):
    piece = pl.BlockSpec((1, SUB, COLS), lambda n: (n, 0, 0))
    first = pl.BlockSpec((SUB, COLS), lambda n: (0, PER * part + n))
    block = pl.BlockSpec((NY, SUB, COLS), lambda n: (0, 0, PER * part + n))
    more = [] if earlier is None else [earlier]
    return pl.pallas_call(
        final_kernel,
        grid=(PER,),
        in_specs=[block] + [piece] * 4 + [first] * 4 + [pl.BlockSpec(memory_space=pl.ANY)] * len(more),
        out_specs=block,
        out_shape=jax.ShapeDtypeStruct((NY, SUB, D), F32),
        input_output_aliases={9: 0} if more else {},
        compiler_params=pltpu.CompilerParams(vmem_limit_bytes=12 << 20),
        cost_estimate=pl.CostEstimate(flops=1, bytes_accessed=1, transcendentals=0),
        name="final_sum",
    )(latents.reshape(NY, SUB, D), *pieces, *firsts, *more)


def barrier(*arrays):
    return lax.optimization_barrier(arrays)


def per_device(latents, timesteps, mod_weight, qkv_weight, qk_gain, out_weight, block_list):
    step = lax.axis_index("tm")
    z, y = step // NY, step % NY

    piece = lax.dynamic_slice(out_weight, (z * DEEP, y * COLS), (DEEP, COLS))
    pieces = [shift_x(piece, d) for d in range(1, NX)]
    first_core = lax.axis_index("seq") % 2 == 0
    y_is = [y == n for n in range(NY)]
    z_is = [z == n for n in range(NZ)]
    z_from = [z >= n for n in range(NZ)]
    z_odd = z % 2 == 1
    modulated = modulate(latents, timesteps, mod_weight)
    modulated, pieces, first_core, y_is, z_is, z_from, z_odd = barrier(
        modulated, pieces, first_core, y_is, z_is, z_from, z_odd
    )
    gathered = lax.all_gather(jnp.stack(pieces), "tm").reshape(NZ, NY, NX - 1, DEEP, COLS)

    twin = swap_core(modulated)
    before = shift_x(modulated, 1)
    after = shift_x(modulated, -1)

    twin, current, weight, gate_weight = barrier(twin, latents[0], qkv_weight, mod_weight)
    gates = row_gates(timesteps, gate_weight)
    half = current.astype(jnp.float16).reshape(NY, SUB, D)
    parts = [shift_y(half[to], to) for to in range(1, NY)]
    held = qkv_tiles([modulated, twin], ((0, 0), (0, 1)), qk_gain, weight, None)

    before, after, held, parts, half, gates = barrier(before, after, held, parts, half, gates)
    far = opposite_x(first_core, before, after)
    quarter = half[0]
    for to in range(1, NY):
        quarter = jnp.where(y_is[to], parts[to - 1], quarter)
    got = shift_z(quarter, 2)
    near = [after, swap_core(after), before, swap_core(before)]
    places = ((1, 0), (1, 1), (3, 0), (3, 1))
    held = qkv_tiles(near, places, qk_gain, weight, held)
    far, held, quarter, got = barrier(far, held, quarter, got)
    quarter = jnp.where(z_is[2], got, quarter)
    far_twin = swap_core(far)
    held = qkv_tiles([far], ((2, 0),), qk_gain, weight, held)
    held = qkv_tiles([far_twin], ((2, 1),), qk_gain, weight, held)

    arrived = [None] * NX
    for d in (2, 1, 3, 0):
        if d == 0:
            held, arrived[2], quarter = barrier(held, arrived[2], quarter)
            got = shift_z(quarter, 1)
        attended = attend_tile(block_list, d, held)
        arrived[d] = shift_x(attended, d) if d else attended

    arrived, gathered, own_weight = barrier(arrived, gathered, out_weight)
    pieces = pack(arrived)
    pieces = [shift_y(send, d) if d else send for d, send in enumerate(pieces)]
    own_weight, gathered = load(own_weight, gathered)

    pieces[1], got, quarter = barrier(pieces[1], got, quarter)
    quarter = jnp.where(z_odd, got, quarter)
    firsts = [shift_y(quarter, -d) if d else quarter for d in range(NY)]
    own, other = out_project(pieces, own_weight, gathered, gates)
    other = swap_core(other)

    result = None
    for part in range(PARTS):
        parts, total = row_prefix(part, own, other)
        base = sum(
            jnp.where(z_from[by], shift_z(total, by).astype(F32), 0.0) for by in range(1, NZ)
        )
        back = []
        for d in range(NY):
            send = (parts[d] + base).astype(BF)
            back.append(shift_y(send, -d) if d else send)
        if part == 0:
            firsts = [first.astype(F32) for first in firsts]
        result = final_sum(part, latents, back, firsts, result)
    return result.reshape(1, ROWS, D)


def solution(mesh):
    return jax.shard_map(
        per_device,
        mesh=mesh,
        in_specs=(
            P("tm", "seq", None),
            P(),
            P(),
            P(None, None, "seq"),
            P(),
            P("seq", None),
            P("seq", None, None),
        ),
        out_specs=P("tm", "seq", None),
        check_vma=False,
    )
```

```python
import functools
import math

import jax
import jax.numpy as jnp
from jax import lax
from jax.experimental import pallas as pl
from jax.experimental.pallas import tpu as pltpu
from jax.sharding import PartitionSpec as P

D = 3072
BLOCK = 384
HEAD = 128
LOCAL_HEADS = 3
WIDTH = LOCAL_HEADS * HEAD
NX = 4
NY = 4
NZ = 4
ROWS = 192
SUB = 48
COLS = D // NY
DEEP = WIDTH // NZ
PARTS = 2
PER = NY // PARTS
eps_norm = 1e-06

BF = jnp.bfloat16
F32 = jnp.float32
VMEM = pl.BlockSpec(memory_space=pltpu.VMEM)
SMEM = pl.BlockSpec(memory_space=pltpu.SMEM)


def row_embedding(stamps_ref, row):
    lane = lax.broadcasted_iota(jnp.int32, (8, HEAD), 0)
    stamps = jnp.zeros((8, HEAD), F32)
    for n in range(NY):
        stamps = jnp.where(lane == n, stamps_ref[row * NY + n].astype(F32), stamps)
    place = lax.broadcasted_iota(jnp.int32, (8, HEAD), 1).astype(F32)
    angles = stamps * jnp.exp(-math.log(10000.0) * place / HEAD)
    return jnp.concatenate([jnp.cos(angles), jnp.sin(angles)], axis=1).astype(BF)


def modulate_kernel(stamps_ref, w_hbm, lat_hbm, out_ref, w, lat, held, w_sems, lat_sems):
    step = lax.axis_index("tm")
    row, y = step // NY, step % NY
    lat_copies = [
        pltpu.make_async_copy(
            lat_hbm.at[0, pl.ds(n * SUB, SUB)], lat.at[pl.ds(n * SUB, SUB)], lat_sems.at[n]
        )
        for n in range(4)
    ]
    w_copies = [
        pltpu.make_async_copy(w_hbm.at[:, pl.ds(n * D, D)], w.at[:, pl.ds(n * D, D)], w_sems.at[n])
        for n in range(2)
    ]
    for copy in lat_copies + w_copies:
        copy.start()
    emb = row_embedding(stamps_ref, row)
    for n in range(4):
        lat_copies[n].wait()
        part = slice(n * SUB, (n + 1) * SUB)
        current = lat[part, :]
        centred = current - jnp.mean(current, axis=-1, keepdims=True)
        var = jnp.mean(centred * centred, axis=-1, keepdims=True)
        lat[part, :] = centred * lax.rsqrt(var + eps_norm)
    for n in range(2):
        w_copies[n].wait()
        cols = slice(n * D, (n + 1) * D)
        held[:, cols] = jnp.dot(emb, w[:, cols], preferred_element_type=F32)
    shift = held[pl.ds(y, 1), :D]
    scale = held[pl.ds(y, 1), D:]
    for n in range(4):
        part = slice(n * SUB, (n + 1) * SUB)
        out_ref[part, :] = (lat[part, :] * (1.0 + scale) + shift).astype(BF)


def modulate(latents, timesteps, mod_weight):
    depth = mod_weight.shape[0]
    return pl.pallas_call(
        modulate_kernel,
        in_specs=[SMEM] + [pl.BlockSpec(memory_space=pl.ANY)] * 2,
        out_specs=VMEM,
        out_shape=jax.ShapeDtypeStruct((ROWS, D), BF),
        scratch_shapes=[
            pltpu.VMEM((depth, 2 * D), BF),
            pltpu.VMEM((ROWS, D), F32),
            pltpu.VMEM((8, 2 * D), F32),
            pltpu.SemaphoreType.DMA((2,)),
            pltpu.SemaphoreType.DMA((4,)),
        ],
        compiler_params=pltpu.CompilerParams(vmem_limit_bytes=58 << 20),
        cost_estimate=pl.CostEstimate(
            flops=10 * ROWS * D, bytes_accessed=9_000_000, transcendentals=ROWS
        ),
        name="modulate",
    )(timesteps, mod_weight, latents)


def gate_kernel(stamps_ref, w_ref, gate_ref):
    row = lax.axis_index("tm") // NY
    gates = jnp.dot(row_embedding(stamps_ref, row), w_ref[...], preferred_element_type=F32)
    for n in range(NY):
        delta = (stamps_ref[row * NY + n + 1] - stamps_ref[row * NY + n]).astype(F32) / 1000.0
        gate_ref[n : n + 1, :] = gates[n : n + 1, :] * delta


def row_gates(timesteps, mod_weight):
    return pl.pallas_call(
        gate_kernel,
        grid=(1,),
        in_specs=[SMEM, pl.BlockSpec((mod_weight.shape[0], D), lambda n: (0, 2))],
        out_specs=pl.BlockSpec((NY, D), lambda n: (0, 0)),
        out_shape=jax.ShapeDtypeStruct((NY, D), F32),
        compiler_params=pltpu.CompilerParams(vmem_limit_bytes=10 << 20),
        cost_estimate=pl.CostEstimate(flops=1, bytes_accessed=2_000_000, transcendentals=0),
        name="row_gates",
    )(timesteps, mod_weight)


def shift_x(array, by):
    return lax.ppermute(array, "seq", [(i, (i + 2 * by) % 8) for i in range(8)])


def swap_core(array):
    return lax.ppermute(array, "seq", [(i, i ^ 1) for i in range(8)])


def shift_y(array, by):
    pairs = [(z * NY + y, z * NY + (y + by) % NY) for z in range(NZ) for y in range(NY)]
    return lax.ppermute(array, "tm", pairs)


def opposite_x(first_core, forward, backward):
    send = jnp.where(first_core, forward, backward)
    return lax.ppermute(send, "seq", [(i, (i + 2 - 4 * (i % 2)) % 8) for i in range(8)])


def shift_z(array, by):
    pairs = [(z * NY + y, (z + by) % NZ * NY + y) for z in range(NZ) for y in range(NY)]
    return lax.ppermute(array, "tm", pairs)


def load_kernel(*refs):
    count = (len(refs) - 1) // 2
    sems = refs[-1]
    copies = [pltpu.make_async_copy(refs[n], refs[count + n], sems.at[n]) for n in range(count)]
    for copy in copies:
        copy.start()
    for copy in copies:
        copy.wait()


def load(*arrays):
    return pl.pallas_call(
        load_kernel,
        in_specs=[pl.BlockSpec(memory_space=pl.ANY)] * len(arrays),
        out_specs=[VMEM] * len(arrays),
        out_shape=[jax.ShapeDtypeStruct(a.shape, a.dtype) for a in arrays],
        scratch_shapes=[pltpu.SemaphoreType.DMA((len(arrays),))],
        compiler_params=pltpu.CompilerParams(vmem_limit_bytes=11 << 20),
        cost_estimate=pl.CostEstimate(
            flops=1, bytes_accessed=2 * sum(a.size * 2 for a in arrays), transcendentals=0
        ),
        name="load",
    )(*arrays)


def qkv_kernel(places, *refs):
    parts, (gain_ref, w_ref), out_ref = refs[: len(places)], refs[len(places) :][:2], refs[-1]
    rows = jnp.concatenate([part[...] for part in parts], axis=0) if len(parts) > 1 else parts[0][...]
    blocks = [(kind, h) for kind in range(3) for h in range(LOCAL_HEADS)]
    for n in range(0, len(blocks), 2):
        pair = blocks[n : n + 2]
        weight = [w_ref[kind, :, h * HEAD : (h + 1) * HEAD] for kind, h in pair]
        weight = jnp.concatenate(weight, axis=1) if len(pair) > 1 else weight[0]
        proj = jnp.dot(rows, weight, preferred_element_type=F32)
        for m, (kind, h) in enumerate(pair):
            part = proj[:, m * HEAD : (m + 1) * HEAD]
            if kind < 2:
                inverse = lax.rsqrt(jnp.mean(part * part, axis=-1, keepdims=True) + eps_norm)
                part = part * inverse * gain_ref[kind : kind + 1, :]
            part = part.astype(BF)
            for t, (place, half) in enumerate(places):
                at = slice(half * ROWS, (half + 1) * ROWS)
                out_ref[place, kind, at, h * HEAD : (h + 1) * HEAD] = part[t * ROWS : (t + 1) * ROWS]


def qkv_tiles(parts, places, gain, weight, held):
    earlier = [] if held is None else [held]
    return pl.pallas_call(
        functools.partial(qkv_kernel, places),
        in_specs=[VMEM] * (len(parts) + 2 + len(earlier)),
        out_specs=VMEM,
        out_shape=jax.ShapeDtypeStruct((NX, 3, BLOCK, WIDTH), BF),
        input_output_aliases={len(parts) + 2: 0} if earlier else {},
        compiler_params=pltpu.CompilerParams(vmem_limit_bytes=11 << 20),
        cost_estimate=pl.CostEstimate(
            flops=2 * len(places) * ROWS * D * 3 * WIDTH, bytes_accessed=10_000_000, transcendentals=0
        ),
        name="qkv_tiles",
    )(*parts, gain, weight, *earlier)


def attend_kernel(place, list_ref, held_ref, out_ref):
    x = lax.axis_index("seq") // 2
    factor = 1.0 / math.sqrt(HEAD)
    ones = jnp.ones((BLOCK, HEAD), BF)
    for h in range(LOCAL_HEADS):
        cols = slice(h * HEAD, (h + 1) * HEAD)
        tiles = [(list_ref[h, (x + place) % NX, n] - x) % NX for n in range(3)]
        query = held_ref[place, 0, :, cols]
        scores = [
            lax.dot_general(
                query, held_ref[t, 1, :, cols], (((1,), (1,)), ((), ())), preferred_element_type=F32
            )
            for t in tiles
        ]
        top = functools.reduce(jnp.maximum, [jnp.max(s, axis=-1, keepdims=True) for s in scores])
        total = jnp.zeros((BLOCK, 2 * HEAD), F32)
        for s, t in zip(scores, tiles):
            probs = jnp.exp((s - top) * factor).astype(BF)
            values = jnp.concatenate([held_ref[t, 2, :, cols], ones], axis=1)
            total += jnp.dot(probs, values, preferred_element_type=F32)
        out_ref[:, cols] = (total[:, :HEAD] / total[:, HEAD:]).astype(BF)


def attend_tile(block_list, place, held):
    return pl.pallas_call(
        functools.partial(attend_kernel, place),
        in_specs=[SMEM, VMEM],
        out_specs=VMEM,
        out_shape=jax.ShapeDtypeStruct((BLOCK, WIDTH), BF),
        compiler_params=pltpu.CompilerParams(vmem_limit_bytes=12 << 20),
        cost_estimate=pl.CostEstimate(
            flops=4 * 3 * BLOCK * 3 * BLOCK * HEAD, bytes_accessed=4_000_000, transcendentals=0
        ),
        name="attend_tile",
    )(block_list, held)


def pack_kernel(a0, a1, a2, a3, o0, o1, o2, o3, sems):
    y = lax.axis_index("tm") % NY
    copies = []
    for d, out_ref in enumerate((o0, o1, o2, o3)):
        sub = (y + d) % NY
        for n, a in enumerate((a0, a1, a2, a3)):
            for half in range(2):
                at = pl.multiple_of(half * ROWS + sub * SUB, 16)
                copies.append(
                    pltpu.make_async_copy(
                        a.at[pl.ds(at, SUB)], out_ref.at[n, half], sems.at[d, n, half]
                    )
                )
    for copy in copies:
        copy.start()
    for copy in copies:
        copy.wait()


def pack(arrived):
    return pl.pallas_call(
        pack_kernel,
        in_specs=[pl.BlockSpec(memory_space=pl.ANY)] * NX,
        out_specs=[VMEM] * NY,
        out_shape=[jax.ShapeDtypeStruct((NX, 2, SUB, WIDTH), BF)] * NY,
        scratch_shapes=[pltpu.SemaphoreType.DMA((NY, NX, 2))],
        compiler_params=pltpu.CompilerParams(vmem_limit_bytes=4 << 20),
        cost_estimate=pl.CostEstimate(flops=1, bytes_accessed=40_000_000, transcendentals=0),
        name="pack",
    )(*arrived)


def out_kernel(p0, p1, p2, p3, own_ref, w_ref, gate_ref, mine_ref, other_ref, rows):
    y = lax.axis_index("tm") % NY
    for half in range(2):
        for d in range(NX):
            part = [p[d, half] for p in (p0, p1, p2, p3)]
            at = slice(half * ROWS, (half + 1) * ROWS)
            rows[at, d * WIDTH : (d + 1) * WIDTH] = jnp.concatenate(part, axis=0)

    @pl.loop(0, NY)
    def _(n):
        cols = pl.ds(pl.multiple_of(n * COLS, COLS), COLS)
        block = [own_ref[:, cols]]
        block += [w_ref[z, n, d] for d in range(NX - 1) for z in range(NZ)]
        block = jnp.concatenate(block, axis=0)
        proj = jnp.dot(rows[...], block, preferred_element_type=F32)
        for d in range(NY):
            gate = gate_ref[pl.ds((y - d) % NY, 1), cols]
            mine_ref[n, d] = (proj[d * SUB : (d + 1) * SUB] * gate).astype(BF)
            other_ref[n, d] = (proj[ROWS + d * SUB : ROWS + (d + 1) * SUB] * gate).astype(BF)


def out_project(pieces, own, gathered, gates):
    return pl.pallas_call(
        out_kernel,
        in_specs=[VMEM] * 7,
        out_specs=[VMEM] * 2,
        out_shape=[jax.ShapeDtypeStruct((NY, NY, SUB, COLS), BF)] * 2,
        scratch_shapes=[pltpu.VMEM((2 * ROWS, NX * WIDTH), BF)],
        compiler_params=pltpu.CompilerParams(vmem_limit_bytes=12 << 20),
        cost_estimate=pl.CostEstimate(
            flops=4 * ROWS * NX * WIDTH * D, bytes_accessed=12_000_000, transcendentals=0
        ),
        name="out_project",
    )(*pieces, own, gathered, gates)


def row_kernel(part, own_ref, other_ref, part_ref, total_ref, held):
    y = lax.axis_index("tm") % NY
    for n in range(PER):
        for d in range(NY):
            at = PER * part + n
            held[(y - d) % NY] = own_ref[at, d].astype(F32) + other_ref[at, d].astype(F32)
        held[1] = held[0] + held[1]
        held[2] = held[1] + held[2]
        held[3] = held[2] + held[3]
        total_ref[n] = held[3].astype(BF)
        for d in range(NY):
            part_ref[d, n] = held[(y - d) % NY]


def row_prefix(part, own, other):
    return pl.pallas_call(
        functools.partial(row_kernel, part),
        in_specs=[VMEM] * 2,
        out_specs=[VMEM] * 2,
        out_shape=[
            jax.ShapeDtypeStruct((NY, PER, SUB, COLS), F32),
            jax.ShapeDtypeStruct((PER, SUB, COLS), BF),
        ],
        scratch_shapes=[pltpu.VMEM((NY, SUB, COLS), F32)],
        compiler_params=pltpu.CompilerParams(vmem_limit_bytes=12 << 20),
        cost_estimate=pl.CostEstimate(flops=1, bytes_accessed=2_000_000, transcendentals=0),
        name="row_prefix",
    )(own, other)


def final_kernel(lat_ref, *refs):
    pieces, firsts, out_ref = refs[:4], refs[4:8], refs[-1]
    step = lax.axis_index("tm")
    y = step % NY
    for d in range(NY):
        at = (y + d) % NY
        first = jnp.where(step == 0, lat_ref[at], firsts[d][...])
        out_ref[at] = first + pieces[d][0].astype(F32)


def final_sum(part, latents, pieces, firsts, earlier):
    piece = pl.BlockSpec((1, SUB, COLS), lambda n: (n, 0, 0))
    first = pl.BlockSpec((SUB, COLS), lambda n: (0, PER * part + n))
    block = pl.BlockSpec((NY, SUB, COLS), lambda n: (0, 0, PER * part + n))
    more = [] if earlier is None else [earlier]
    return pl.pallas_call(
        final_kernel,
        grid=(PER,),
        in_specs=[block] + [piece] * 4 + [first] * 4 + [pl.BlockSpec(memory_space=pl.ANY)] * len(more),
        out_specs=block,
        out_shape=jax.ShapeDtypeStruct((NY, SUB, D), F32),
        input_output_aliases={9: 0} if more else {},
        compiler_params=pltpu.CompilerParams(vmem_limit_bytes=12 << 20),
        cost_estimate=pl.CostEstimate(flops=1, bytes_accessed=1, transcendentals=0),
        name="final_sum",
    )(latents.reshape(NY, SUB, D), *pieces, *firsts, *more)


def barrier(*arrays):
    return lax.optimization_barrier(arrays)


def per_device(latents, timesteps, mod_weight, qkv_weight, qk_gain, out_weight, block_list):
    step = lax.axis_index("tm")
    z, y = step // NY, step % NY

    piece = lax.dynamic_slice(out_weight, (z * DEEP, y * COLS), (DEEP, COLS))
    pieces = [shift_x(piece, d) for d in range(1, NX)]
    first_core = lax.axis_index("seq") % 2 == 0
    y_is = [y == n for n in range(NY)]
    z_is = [z == n for n in range(NZ)]
    z_from = [z >= n for n in range(NZ)]
    z_odd = z % 2 == 1
    modulated = modulate(latents, timesteps, mod_weight)
    modulated, pieces, first_core, y_is, z_is, z_from, z_odd = barrier(
        modulated, pieces, first_core, y_is, z_is, z_from, z_odd
    )
    gathered = lax.all_gather(jnp.stack(pieces), "tm").reshape(NZ, NY, NX - 1, DEEP, COLS)

    twin = swap_core(modulated)
    before = shift_x(modulated, 1)
    after = shift_x(modulated, -1)

    twin, current, weight, gate_weight = barrier(twin, latents[0], qkv_weight, mod_weight)
    gates = row_gates(timesteps, gate_weight)
    half = current.astype(jnp.float16).reshape(NY, SUB, D)
    parts = [shift_y(half[to], to) for to in range(1, NY)]
    held = qkv_tiles([modulated, twin], ((0, 0), (0, 1)), qk_gain, weight, None)

    before, after, held, parts, half, gates = barrier(before, after, held, parts, half, gates)
    far = opposite_x(first_core, before, after)
    quarter = half[0]
    for to in range(1, NY):
        quarter = jnp.where(y_is[to], parts[to - 1], quarter)
    got = shift_z(quarter, 2)
    near = [after, swap_core(after), before, swap_core(before)]
    places = ((1, 0), (1, 1), (3, 0), (3, 1))
    held = qkv_tiles(near, places, qk_gain, weight, held)
    far, held, quarter, got = barrier(far, held, quarter, got)
    quarter = jnp.where(z_is[2], got, quarter)
    far_twin = swap_core(far)
    held = qkv_tiles([far], ((2, 0),), qk_gain, weight, held)
    held = qkv_tiles([far_twin], ((2, 1),), qk_gain, weight, held)

    arrived = [None] * NX
    for d in (2, 1, 3, 0):
        if d == 0:
            held, arrived[2], quarter = barrier(held, arrived[2], quarter)
            got = shift_z(quarter, 1)
        attended = attend_tile(block_list, d, held)
        arrived[d] = shift_x(attended, d) if d else attended

    arrived, gathered, own_weight = barrier(arrived, gathered, out_weight)
    pieces = pack(arrived)
    pieces = [shift_y(send, d) if d else send for d, send in enumerate(pieces)]
    own_weight, gathered = load(own_weight, gathered)

    pieces[1], got, quarter = barrier(pieces[1], got, quarter)
    quarter = jnp.where(z_odd, got, quarter)
    firsts = [shift_y(quarter, -d) if d else quarter for d in range(NY)]
    own, other = out_project(pieces, own_weight, gathered, gates)
    other = swap_core(other)

    result = None
    for part in range(PARTS):
        parts, total = row_prefix(part, own, other)
        base = sum(
            jnp.where(z_from[by], shift_z(total, by).astype(F32), 0.0) for by in range(1, NZ)
        )
        back = []
        for d in range(NY):
            send = (parts[d] + base).astype(BF)
            back.append(shift_y(send, -d) if d else send)
        if part == 0:
            firsts = [first.astype(F32) for first in firsts]
        result = final_sum(part, latents, back, firsts, result)
    return result.reshape(1, ROWS, D)


def solution(mesh):
    return jax.shard_map(
        per_device,
        mesh=mesh,
        in_specs=(
            P("tm", "seq", None),
            P(),
            P(),
            P(None, None, "seq"),
            P(),
            P("seq", None),
            P("seq", None, None),
        ),
        out_specs=P("tm", "seq", None),
        check_vma=False,
    )
```

```python
import functools
import math

import jax
import jax.numpy as jnp
from jax import lax
from jax.experimental import pallas as pl
from jax.experimental.pallas import tpu as pltpu
from jax.sharding import PartitionSpec as P

D = 3072
BLOCK = 384
HEAD = 128
LOCAL_HEADS = 3
WIDTH = LOCAL_HEADS * HEAD
NX = 4
NY = 4
NZ = 4
ROWS = 192
SUB = 48
COLS = D // NY
DEEP = WIDTH // NZ
PARTS = 2
PER = NY // PARTS
eps_norm = 1e-06

BF = jnp.bfloat16
F32 = jnp.float32
VMEM = pl.BlockSpec(memory_space=pltpu.VMEM)
SMEM = pl.BlockSpec(memory_space=pltpu.SMEM)


def row_embedding(stamps_ref, row):
    lane = lax.broadcasted_iota(jnp.int32, (8, HEAD), 0)
    stamps = jnp.zeros((8, HEAD), F32)
    for n in range(NY):
        stamps = jnp.where(lane == n, stamps_ref[row * NY + n].astype(F32), stamps)
    place = lax.broadcasted_iota(jnp.int32, (8, HEAD), 1).astype(F32)
    angles = stamps * jnp.exp(-math.log(10000.0) * place / HEAD)
    return jnp.concatenate([jnp.cos(angles), jnp.sin(angles)], axis=1).astype(BF)


def modulate_kernel(stamps_ref, w_hbm, lat_hbm, out_ref, w, lat, held, w_sems, lat_sems):
    step = lax.axis_index("tm")
    row, y = step // NY, step % NY
    lat_copies = [
        pltpu.make_async_copy(
            lat_hbm.at[0, pl.ds(n * SUB, SUB)], lat.at[pl.ds(n * SUB, SUB)], lat_sems.at[n]
        )
        for n in range(4)
    ]
    w_copies = [
        pltpu.make_async_copy(w_hbm.at[:, pl.ds(n * D, D)], w.at[:, pl.ds(n * D, D)], w_sems.at[n])
        for n in range(2)
    ]
    for copy in lat_copies + w_copies:
        copy.start()
    emb = row_embedding(stamps_ref, row)
    for n in range(4):
        lat_copies[n].wait()
        part = slice(n * SUB, (n + 1) * SUB)
        current = lat[part, :]
        centred = current - jnp.mean(current, axis=-1, keepdims=True)
        var = jnp.mean(centred * centred, axis=-1, keepdims=True)
        lat[part, :] = centred * lax.rsqrt(var + eps_norm)
    for n in range(2):
        w_copies[n].wait()
        cols = slice(n * D, (n + 1) * D)
        held[:, cols] = jnp.dot(emb, w[:, cols], preferred_element_type=F32)
    shift = held[pl.ds(y, 1), :D]
    scale = held[pl.ds(y, 1), D:]
    for n in range(4):
        part = slice(n * SUB, (n + 1) * SUB)
        out_ref[part, :] = (lat[part, :] * (1.0 + scale) + shift).astype(BF)


def modulate(latents, timesteps, mod_weight):
    depth = mod_weight.shape[0]
    return pl.pallas_call(
        modulate_kernel,
        in_specs=[SMEM] + [pl.BlockSpec(memory_space=pl.ANY)] * 2,
        out_specs=VMEM,
        out_shape=jax.ShapeDtypeStruct((ROWS, D), BF),
        scratch_shapes=[
            pltpu.VMEM((depth, 2 * D), BF),
            pltpu.VMEM((ROWS, D), F32),
            pltpu.VMEM((8, 2 * D), F32),
            pltpu.SemaphoreType.DMA((2,)),
            pltpu.SemaphoreType.DMA((4,)),
        ],
        compiler_params=pltpu.CompilerParams(vmem_limit_bytes=57 << 20),
        cost_estimate=pl.CostEstimate(
            flops=10 * ROWS * D, bytes_accessed=9_000_000, transcendentals=ROWS
        ),
        name="modulate",
    )(timesteps, mod_weight, latents)


def gate_kernel(stamps_ref, w_ref, gate_ref):
    row = lax.axis_index("tm") // NY
    gates = jnp.dot(row_embedding(stamps_ref, row), w_ref[...], preferred_element_type=F32)
    for n in range(NY):
        delta = (stamps_ref[row * NY + n + 1] - stamps_ref[row * NY + n]).astype(F32) / 1000.0
        gate_ref[n : n + 1, :] = gates[n : n + 1, :] * delta


def row_gates(timesteps, mod_weight):
    return pl.pallas_call(
        gate_kernel,
        grid=(1,),
        in_specs=[SMEM, pl.BlockSpec((mod_weight.shape[0], D), lambda n: (0, 2))],
        out_specs=pl.BlockSpec((NY, D), lambda n: (0, 0)),
        out_shape=jax.ShapeDtypeStruct((NY, D), F32),
        compiler_params=pltpu.CompilerParams(vmem_limit_bytes=10 << 20),
        cost_estimate=pl.CostEstimate(flops=1, bytes_accessed=2_000_000, transcendentals=0),
        name="row_gates",
    )(timesteps, mod_weight)


def shift_x(array, by):
    return lax.ppermute(array, "seq", [(i, (i + 2 * by) % 8) for i in range(8)])


def swap_core(array):
    return lax.ppermute(array, "seq", [(i, i ^ 1) for i in range(8)])


def shift_y(array, by):
    pairs = [(z * NY + y, z * NY + (y + by) % NY) for z in range(NZ) for y in range(NY)]
    return lax.ppermute(array, "tm", pairs)


def opposite_x(first_core, forward, backward):
    send = jnp.where(first_core, forward, backward)
    return lax.ppermute(send, "seq", [(i, (i + 2 - 4 * (i % 2)) % 8) for i in range(8)])


def shift_z(array, by):
    pairs = [(z * NY + y, (z + by) % NZ * NY + y) for z in range(NZ) for y in range(NY)]
    return lax.ppermute(array, "tm", pairs)


def load_kernel(*refs):
    count = (len(refs) - 1) // 2
    sems = refs[-1]
    copies = [pltpu.make_async_copy(refs[n], refs[count + n], sems.at[n]) for n in range(count)]
    for copy in copies:
        copy.start()
    for copy in copies:
        copy.wait()


def load(*arrays):
    return pl.pallas_call(
        load_kernel,
        in_specs=[pl.BlockSpec(memory_space=pl.ANY)] * len(arrays),
        out_specs=[VMEM] * len(arrays),
        out_shape=[jax.ShapeDtypeStruct(a.shape, a.dtype) for a in arrays],
        scratch_shapes=[pltpu.SemaphoreType.DMA((len(arrays),))],
        compiler_params=pltpu.CompilerParams(vmem_limit_bytes=16 << 20),
        cost_estimate=pl.CostEstimate(
            flops=1, bytes_accessed=2 * sum(a.size * 2 for a in arrays), transcendentals=0
        ),
        name="load",
    )(*arrays)


def qkv_kernel(places, *refs):
    parts, (gain_ref, w_ref), out_ref = refs[: len(places)], refs[len(places) :][:2], refs[-1]
    rows = jnp.concatenate([part[...] for part in parts], axis=0) if len(parts) > 1 else parts[0][...]
    blocks = [(kind, h) for kind in range(3) for h in range(LOCAL_HEADS)]
    for n in range(0, len(blocks), 2):
        pair = blocks[n : n + 2]
        weight = [w_ref[kind, :, h * HEAD : (h + 1) * HEAD] for kind, h in pair]
        weight = jnp.concatenate(weight, axis=1) if len(pair) > 1 else weight[0]
        proj = jnp.dot(rows, weight, preferred_element_type=F32)
        for m, (kind, h) in enumerate(pair):
            part = proj[:, m * HEAD : (m + 1) * HEAD]
            if kind < 2:
                inverse = lax.rsqrt(jnp.mean(part * part, axis=-1, keepdims=True) + eps_norm)
                part = part * inverse * gain_ref[kind : kind + 1, :]
            part = part.astype(BF)
            for t, (place, half) in enumerate(places):
                at = slice(half * ROWS, (half + 1) * ROWS)
                out_ref[place, kind, at, h * HEAD : (h + 1) * HEAD] = part[t * ROWS : (t + 1) * ROWS]


def qkv_tiles(parts, places, gain, weight, held):
    earlier = [] if held is None else [held]
    return pl.pallas_call(
        functools.partial(qkv_kernel, places),
        in_specs=[VMEM] * (len(parts) + 2 + len(earlier)),
        out_specs=VMEM,
        out_shape=jax.ShapeDtypeStruct((NX, 3, BLOCK, WIDTH), BF),
        input_output_aliases={len(parts) + 2: 0} if earlier else {},
        compiler_params=pltpu.CompilerParams(vmem_limit_bytes=16 << 20),
        cost_estimate=pl.CostEstimate(
            flops=2 * len(places) * ROWS * D * 3 * WIDTH, bytes_accessed=10_000_000, transcendentals=0
        ),
        name="qkv_tiles",
    )(*parts, gain, weight, *earlier)


def attend_kernel(place, list_ref, held_ref, out_ref):
    x = lax.axis_index("seq") // 2
    factor = 1.0 / math.sqrt(HEAD)
    ones = jnp.ones((BLOCK, HEAD), BF)
    for h in range(LOCAL_HEADS):
        cols = slice(h * HEAD, (h + 1) * HEAD)
        tiles = [(list_ref[h, (x + place) % NX, n] - x) % NX for n in range(3)]
        query = held_ref[place, 0, :, cols]
        scores = [
            lax.dot_general(
                query, held_ref[t, 1, :, cols], (((1,), (1,)), ((), ())), preferred_element_type=F32
            )
            for t in tiles
        ]
        top = functools.reduce(jnp.maximum, [jnp.max(s, axis=-1, keepdims=True) for s in scores])
        total = jnp.zeros((BLOCK, 2 * HEAD), F32)
        for s, t in zip(scores, tiles):
            probs = jnp.exp((s - top) * factor).astype(BF)
            values = jnp.concatenate([held_ref[t, 2, :, cols], ones], axis=1)
            total += jnp.dot(probs, values, preferred_element_type=F32)
        out_ref[:, cols] = (total[:, :HEAD] / total[:, HEAD:]).astype(BF)


def attend_tile(block_list, place, held):
    return pl.pallas_call(
        functools.partial(attend_kernel, place),
        in_specs=[SMEM, VMEM],
        out_specs=VMEM,
        out_shape=jax.ShapeDtypeStruct((BLOCK, WIDTH), BF),
        compiler_params=pltpu.CompilerParams(vmem_limit_bytes=12 << 20),
        cost_estimate=pl.CostEstimate(
            flops=4 * 3 * BLOCK * 3 * BLOCK * HEAD, bytes_accessed=4_000_000, transcendentals=0
        ),
        name="attend_tile",
    )(block_list, held)


def pack_kernel(a0, a1, a2, a3, o0, o1, o2, o3, sems):
    y = lax.axis_index("tm") % NY
    copies = []
    for d, out_ref in enumerate((o0, o1, o2, o3)):
        sub = (y + d) % NY
        for n, a in enumerate((a0, a1, a2, a3)):
            for half in range(2):
                at = pl.multiple_of(half * ROWS + sub * SUB, 16)
                copies.append(
                    pltpu.make_async_copy(
                        a.at[pl.ds(at, SUB)], out_ref.at[n, half], sems.at[d, n, half]
                    )
                )
    for copy in copies:
        copy.start()
    for copy in copies:
        copy.wait()


def pack(arrived):
    return pl.pallas_call(
        pack_kernel,
        in_specs=[pl.BlockSpec(memory_space=pl.ANY)] * NX,
        out_specs=[VMEM] * NY,
        out_shape=[jax.ShapeDtypeStruct((NX, 2, SUB, WIDTH), BF)] * NY,
        scratch_shapes=[pltpu.SemaphoreType.DMA((NY, NX, 2))],
        compiler_params=pltpu.CompilerParams(vmem_limit_bytes=4 << 20),
        cost_estimate=pl.CostEstimate(flops=1, bytes_accessed=40_000_000, transcendentals=0),
        name="pack",
    )(*arrived)


def out_kernel(p0, p1, p2, p3, own_ref, w_ref, gate_ref, mine_ref, other_ref, rows):
    y = lax.axis_index("tm") % NY
    for half in range(2):
        for d in range(NX):
            part = [p[d, half] for p in (p0, p1, p2, p3)]
            at = slice(half * ROWS, (half + 1) * ROWS)
            rows[at, d * WIDTH : (d + 1) * WIDTH] = jnp.concatenate(part, axis=0)
    for n in range(NY):
        cols = slice(n * COLS, (n + 1) * COLS)
        block = [own_ref[:, cols]]
        block += [w_ref[z, n, d] for d in range(NX - 1) for z in range(NZ)]
        block = jnp.concatenate(block, axis=0)
        proj = jnp.dot(rows[...], block, preferred_element_type=F32)
        for d in range(NY):
            gate = gate_ref[pl.ds((y - d) % NY, 1), cols]
            mine_ref[n, d] = (proj[d * SUB : (d + 1) * SUB] * gate).astype(BF)
            other_ref[n, d] = (proj[ROWS + d * SUB : ROWS + (d + 1) * SUB] * gate).astype(BF)


def out_project(pieces, own, gathered, gates):
    return pl.pallas_call(
        out_kernel,
        in_specs=[VMEM] * 7,
        out_specs=[VMEM] * 2,
        out_shape=[jax.ShapeDtypeStruct((NY, NY, SUB, COLS), BF)] * 2,
        scratch_shapes=[pltpu.VMEM((2 * ROWS, NX * WIDTH), BF)],
        compiler_params=pltpu.CompilerParams(vmem_limit_bytes=12 << 20),
        cost_estimate=pl.CostEstimate(
            flops=4 * ROWS * NX * WIDTH * D, bytes_accessed=12_000_000, transcendentals=0
        ),
        name="out_project",
    )(*pieces, own, gathered, gates)


def row_kernel(part, own_ref, other_ref, part_ref, total_ref, held):
    y = lax.axis_index("tm") % NY
    for n in range(PER):
        for d in range(NY):
            at = PER * part + n
            held[(y - d) % NY] = own_ref[at, d].astype(F32) + other_ref[at, d].astype(F32)
        held[1] = held[0] + held[1]
        held[2] = held[1] + held[2]
        held[3] = held[2] + held[3]
        total_ref[n] = held[3].astype(BF)
        for d in range(NY):
            part_ref[d, n] = held[(y - d) % NY]


def row_prefix(part, own, other):
    return pl.pallas_call(
        functools.partial(row_kernel, part),
        in_specs=[VMEM] * 2,
        out_specs=[VMEM] * 2,
        out_shape=[
            jax.ShapeDtypeStruct((NY, PER, SUB, COLS), F32),
            jax.ShapeDtypeStruct((PER, SUB, COLS), BF),
        ],
        scratch_shapes=[pltpu.VMEM((NY, SUB, COLS), F32)],
        compiler_params=pltpu.CompilerParams(vmem_limit_bytes=12 << 20),
        cost_estimate=pl.CostEstimate(flops=1, bytes_accessed=2_000_000, transcendentals=0),
        name="row_prefix",
    )(own, other)


def final_kernel(lat_ref, *refs):
    pieces, firsts, out_ref = refs[:4], refs[4:8], refs[-1]
    step = lax.axis_index("tm")
    y = step % NY
    for d in range(NY):
        at = (y + d) % NY
        first = jnp.where(step == 0, lat_ref[at], firsts[d][...])
        out_ref[at] = first + pieces[d][0].astype(F32)


def final_sum(part, latents, pieces, firsts, earlier):
    piece = pl.BlockSpec((1, SUB, COLS), lambda n: (n, 0, 0))
    first = pl.BlockSpec((SUB, COLS), lambda n: (0, PER * part + n))
    block = pl.BlockSpec((NY, SUB, COLS), lambda n: (0, 0, PER * part + n))
    more = [] if earlier is None else [earlier]
    return pl.pallas_call(
        final_kernel,
        grid=(PER,),
        in_specs=[block] + [piece] * 4 + [first] * 4 + [pl.BlockSpec(memory_space=pl.ANY)] * len(more),
        out_specs=block,
        out_shape=jax.ShapeDtypeStruct((NY, SUB, D), F32),
        input_output_aliases={9: 0} if more else {},
        compiler_params=pltpu.CompilerParams(vmem_limit_bytes=12 << 20),
        cost_estimate=pl.CostEstimate(flops=1, bytes_accessed=1, transcendentals=0),
        name="final_sum",
    )(latents.reshape(NY, SUB, D), *pieces, *firsts, *more)


def barrier(*arrays):
    return lax.optimization_barrier(arrays)


def per_device(latents, timesteps, mod_weight, qkv_weight, qk_gain, out_weight, block_list):
    step = lax.axis_index("tm")
    z, y = step // NY, step % NY

    piece = lax.dynamic_slice(out_weight, (z * DEEP, y * COLS), (DEEP, COLS))
    pieces = [shift_x(piece, d) for d in range(1, NX)]
    first_core = lax.axis_index("seq") % 2 == 0
    y_is = [y == n for n in range(NY)]
    z_is = [z == n for n in range(NZ)]
    z_from = [z >= n for n in range(NZ)]
    z_odd = z % 2 == 1
    modulated = modulate(latents, timesteps, mod_weight)
    modulated, pieces, first_core, y_is, z_is, z_from, z_odd = barrier(
        modulated, pieces, first_core, y_is, z_is, z_from, z_odd
    )
    gathered = lax.all_gather(jnp.stack(pieces), "tm").reshape(NZ, NY, NX - 1, DEEP, COLS)

    twin = swap_core(modulated)
    before = shift_x(modulated, 1)
    after = shift_x(modulated, -1)

    twin, current, weight, gate_weight = barrier(twin, latents[0], qkv_weight, mod_weight)
    gates = row_gates(timesteps, gate_weight)
    half = current.astype(jnp.float16).reshape(NY, SUB, D)
    parts = [shift_y(half[to], to) for to in range(1, NY)]

    before, after, parts, half, gates = barrier(before, after, parts, half, gates)
    far = opposite_x(first_core, before, after)
    quarter = half[0]
    for to in range(1, NY):
        quarter = jnp.where(y_is[to], parts[to - 1], quarter)
    got = shift_z(quarter, 2)
    near = [modulated, twin, after, swap_core(after), before, swap_core(before)]
    places = ((0, 0), (0, 1), (1, 0), (1, 1), (3, 0), (3, 1))
    held = qkv_tiles(near, places, qk_gain, weight, None)
    far, held, quarter, got = barrier(far, held, quarter, got)
    quarter = jnp.where(z_is[2], got, quarter)
    far_twin = swap_core(far)
    held = qkv_tiles([far], ((2, 0),), qk_gain, weight, held)
    held = qkv_tiles([far_twin], ((2, 1),), qk_gain, weight, held)

    arrived = [None] * NX
    for d in (2, 1, 3, 0):
        if d == 0:
            held, arrived[2], quarter = barrier(held, arrived[2], quarter)
            got = shift_z(quarter, 1)
        attended = attend_tile(block_list, d, held)
        arrived[d] = shift_x(attended, d) if d else attended

    arrived, gathered, own_weight = barrier(arrived, gathered, out_weight)
    pieces = pack(arrived)
    pieces = [shift_y(send, d) if d else send for d, send in enumerate(pieces)]
    own_weight, gathered = load(own_weight, gathered)

    pieces[1], got, quarter = barrier(pieces[1], got, quarter)
    quarter = jnp.where(z_odd, got, quarter)
    firsts = [shift_y(quarter, -d) if d else quarter for d in range(NY)]
    own, other = out_project(pieces, own_weight, gathered, gates)
    other = swap_core(other)

    result = None
    for part in range(PARTS):
        parts, total = row_prefix(part, own, other)
        base = sum(
            jnp.where(z_from[by], shift_z(total, by).astype(F32), 0.0) for by in range(1, NZ)
        )
        back = []
        for d in range(NY):
            send = (parts[d] + base).astype(BF)
            back.append(shift_y(send, -d) if d else send)
        if part == 0:
            firsts = [first.astype(F32) for first in firsts]
        result = final_sum(part, latents, back, firsts, result)
    return result.reshape(1, ROWS, D)


def solution(mesh):
    return jax.shard_map(
        per_device,
        mesh=mesh,
        in_specs=(
            P("tm", "seq", None),
            P(),
            P(),
            P(None, None, "seq"),
            P(),
            P("seq", None),
            P("seq", None, None),
        ),
        out_specs=P("tm", "seq", None),
        check_vma=False,
    )
```

```python
import functools
import math

import jax
import jax.numpy as jnp
from jax import lax
from jax.experimental import pallas as pl
from jax.experimental.pallas import tpu as pltpu
from jax.sharding import PartitionSpec as P

D = 3072
BLOCK = 384
HEAD = 128
LOCAL_HEADS = 3
WIDTH = LOCAL_HEADS * HEAD
NX = 4
NY = 4
NZ = 4
ROWS = 192
SUB = 48
COLS = D // NY
DEEP = WIDTH // NZ
PARTS = 2
PER = NY // PARTS
eps_norm = 1e-06

BF = jnp.bfloat16
F32 = jnp.float32
VMEM = pl.BlockSpec(memory_space=pltpu.VMEM)
SMEM = pl.BlockSpec(memory_space=pltpu.SMEM)


def row_embedding(stamps_ref, row):
    lane = lax.broadcasted_iota(jnp.int32, (8, HEAD), 0)
    stamps = jnp.zeros((8, HEAD), F32)
    for n in range(NY):
        stamps = jnp.where(lane == n, stamps_ref[row * NY + n].astype(F32), stamps)
    place = lax.broadcasted_iota(jnp.int32, (8, HEAD), 1).astype(F32)
    angles = stamps * jnp.exp(-math.log(10000.0) * place / HEAD)
    return jnp.concatenate([jnp.cos(angles), jnp.sin(angles)], axis=1).astype(BF)


def modulate_kernel(stamps_ref, w_hbm, lat_hbm, out_ref, w, lat, held, w_sems, lat_sems):
    step = lax.axis_index("tm")
    row, y = step // NY, step % NY
    lat_copies = [
        pltpu.make_async_copy(
            lat_hbm.at[0, pl.ds(n * SUB, SUB)], lat.at[pl.ds(n * SUB, SUB)], lat_sems.at[n]
        )
        for n in range(4)
    ]
    w_copies = [
        pltpu.make_async_copy(w_hbm.at[:, pl.ds(n * D, D)], w.at[:, pl.ds(n * D, D)], w_sems.at[n])
        for n in range(2)
    ]
    for copy in lat_copies + w_copies:
        copy.start()
    emb = row_embedding(stamps_ref, row)
    for n in range(4):
        lat_copies[n].wait()
        part = slice(n * SUB, (n + 1) * SUB)
        current = lat[part, :]
        centred = current - jnp.mean(current, axis=-1, keepdims=True)
        var = jnp.mean(centred * centred, axis=-1, keepdims=True)
        lat[part, :] = centred * lax.rsqrt(var + eps_norm)
    for n in range(2):
        w_copies[n].wait()
        cols = slice(n * D, (n + 1) * D)
        held[:, cols] = jnp.dot(emb, w[:, cols], preferred_element_type=F32)
    shift = held[pl.ds(y, 1), :D]
    scale = held[pl.ds(y, 1), D:]
    for n in range(4):
        part = slice(n * SUB, (n + 1) * SUB)
        out_ref[part, :] = (lat[part, :] * (1.0 + scale) + shift).astype(BF)


def modulate(latents, timesteps, mod_weight):
    depth = mod_weight.shape[0]
    return pl.pallas_call(
        modulate_kernel,
        in_specs=[SMEM] + [pl.BlockSpec(memory_space=pl.ANY)] * 2,
        out_specs=VMEM,
        out_shape=jax.ShapeDtypeStruct((ROWS, D), BF),
        scratch_shapes=[
            pltpu.VMEM((depth, 2 * D), BF),
            pltpu.VMEM((ROWS, D), F32),
            pltpu.VMEM((8, 2 * D), F32),
            pltpu.SemaphoreType.DMA((2,)),
            pltpu.SemaphoreType.DMA((4,)),
        ],
        compiler_params=pltpu.CompilerParams(vmem_limit_bytes=58 << 20),
        cost_estimate=pl.CostEstimate(
            flops=10 * ROWS * D, bytes_accessed=9_000_000, transcendentals=ROWS
        ),
        name="modulate",
    )(timesteps, mod_weight, latents)


def gate_kernel(stamps_ref, w_ref, gate_ref):
    row = lax.axis_index("tm") // NY
    gates = jnp.dot(row_embedding(stamps_ref, row), w_ref[...], preferred_element_type=F32)
    for n in range(NY):
        delta = (stamps_ref[row * NY + n + 1] - stamps_ref[row * NY + n]).astype(F32) / 1000.0
        gate_ref[n : n + 1, :] = gates[n : n + 1, :] * delta


def row_gates(timesteps, mod_weight):
    return pl.pallas_call(
        gate_kernel,
        grid=(1,),
        in_specs=[SMEM, pl.BlockSpec((mod_weight.shape[0], D), lambda n: (0, 2))],
        out_specs=pl.BlockSpec((NY, D), lambda n: (0, 0)),
        out_shape=jax.ShapeDtypeStruct((NY, D), F32),
        compiler_params=pltpu.CompilerParams(vmem_limit_bytes=10 << 20),
        cost_estimate=pl.CostEstimate(flops=1, bytes_accessed=2_000_000, transcendentals=0),
        name="row_gates",
    )(timesteps, mod_weight)


def shift_x(array, by):
    return lax.ppermute(array, "seq", [(i, (i + 2 * by) % 8) for i in range(8)])


def swap_core(array):
    return lax.ppermute(array, "seq", [(i, i ^ 1) for i in range(8)])


def shift_y(array, by):
    pairs = [(z * NY + y, z * NY + (y + by) % NY) for z in range(NZ) for y in range(NY)]
    return lax.ppermute(array, "tm", pairs)


def opposite_x(first_core, forward, backward):
    send = jnp.where(first_core, forward, backward)
    return lax.ppermute(send, "seq", [(i, (i + 2 - 4 * (i % 2)) % 8) for i in range(8)])


def shift_z(array, by):
    pairs = [(z * NY + y, (z + by) % NZ * NY + y) for z in range(NZ) for y in range(NY)]
    return lax.ppermute(array, "tm", pairs)


def load_kernel(*refs):
    count = (len(refs) - 1) // 2
    sems = refs[-1]
    copies = [pltpu.make_async_copy(refs[n], refs[count + n], sems.at[n]) for n in range(count)]
    for copy in copies:
        copy.start()
    for copy in copies:
        copy.wait()


def load(*arrays):
    return pl.pallas_call(
        load_kernel,
        in_specs=[pl.BlockSpec(memory_space=pl.ANY)] * len(arrays),
        out_specs=[VMEM] * len(arrays),
        out_shape=[jax.ShapeDtypeStruct(a.shape, a.dtype) for a in arrays],
        scratch_shapes=[pltpu.SemaphoreType.DMA((len(arrays),))],
        compiler_params=pltpu.CompilerParams(vmem_limit_bytes=11 << 20),
        cost_estimate=pl.CostEstimate(
            flops=1, bytes_accessed=2 * sum(a.size * 2 for a in arrays), transcendentals=0
        ),
        name="load",
    )(*arrays)


def qkv_kernel(places, *refs):
    parts, (gain_ref, w_ref), out_ref = refs[: len(places)], refs[len(places) :][:2], refs[-1]
    rows = jnp.concatenate([part[...] for part in parts], axis=0) if len(parts) > 1 else parts[0][...]
    blocks = [(kind, h) for kind in range(3) for h in range(LOCAL_HEADS)]
    for n in range(0, len(blocks), 2):
        pair = blocks[n : n + 2]
        weight = [w_ref[kind, :, h * HEAD : (h + 1) * HEAD] for kind, h in pair]
        weight = jnp.concatenate(weight, axis=1) if len(pair) > 1 else weight[0]
        proj = jnp.dot(rows, weight, preferred_element_type=F32)
        for m, (kind, h) in enumerate(pair):
            part = proj[:, m * HEAD : (m + 1) * HEAD]
            if kind < 2:
                inverse = lax.rsqrt(jnp.mean(part * part, axis=-1, keepdims=True) + eps_norm)
                part = part * inverse * gain_ref[kind : kind + 1, :]
            part = part.astype(BF)
            for t, (place, half) in enumerate(places):
                at = slice(half * ROWS, (half + 1) * ROWS)
                out_ref[place, kind, at, h * HEAD : (h + 1) * HEAD] = part[t * ROWS : (t + 1) * ROWS]


def qkv_tiles(parts, places, gain, weight, held):
    earlier = [] if held is None else [held]
    return pl.pallas_call(
        functools.partial(qkv_kernel, places),
        in_specs=[VMEM] * (len(parts) + 2 + len(earlier)),
        out_specs=VMEM,
        out_shape=jax.ShapeDtypeStruct((NX, 3, BLOCK, WIDTH), BF),
        input_output_aliases={len(parts) + 2: 0} if earlier else {},
        compiler_params=pltpu.CompilerParams(vmem_limit_bytes=11 << 20),
        cost_estimate=pl.CostEstimate(
            flops=2 * len(places) * ROWS * D * 3 * WIDTH, bytes_accessed=10_000_000, transcendentals=0
        ),
        name="qkv_tiles",
    )(*parts, gain, weight, *earlier)


def attend_kernel(place, list_ref, held_ref, out_ref):
    x = lax.axis_index("seq") // 2
    factor = 1.0 / math.sqrt(HEAD)
    ones = jnp.ones((BLOCK, HEAD), BF)
    for h in range(LOCAL_HEADS):
        cols = slice(h * HEAD, (h + 1) * HEAD)
        tiles = [(list_ref[h, (x + place) % NX, n] - x) % NX for n in range(3)]
        query = held_ref[place, 0, :, cols]
        scores = [
            lax.dot_general(
                query, held_ref[t, 1, :, cols], (((1,), (1,)), ((), ())), preferred_element_type=F32
            )
            for t in tiles
        ]
        top = functools.reduce(jnp.maximum, [jnp.max(s, axis=-1, keepdims=True) for s in scores])
        total = jnp.zeros((BLOCK, 2 * HEAD), F32)
        for s, t in zip(scores, tiles):
            probs = jnp.exp((s - top) * factor).astype(BF)
            values = jnp.concatenate([held_ref[t, 2, :, cols], ones], axis=1)
            total += jnp.dot(probs, values, preferred_element_type=F32)
        out_ref[:, cols] = (total[:, :HEAD] / total[:, HEAD:]).astype(BF)


def attend_tile(block_list, place, held):
    return pl.pallas_call(
        functools.partial(attend_kernel, place),
        in_specs=[SMEM, VMEM],
        out_specs=VMEM,
        out_shape=jax.ShapeDtypeStruct((BLOCK, WIDTH), BF),
        compiler_params=pltpu.CompilerParams(vmem_limit_bytes=12 << 20),
        cost_estimate=pl.CostEstimate(
            flops=4 * 3 * BLOCK * 3 * BLOCK * HEAD, bytes_accessed=4_000_000, transcendentals=0
        ),
        name="attend_tile",
    )(block_list, held)


def pack_kernel(a0, a1, a2, a3, o0, o1, o2, o3, sems):
    y = lax.axis_index("tm") % NY
    copies = []
    for d, out_ref in enumerate((o0, o1, o2, o3)):
        sub = (y + d) % NY
        for n, a in enumerate((a0, a1, a2, a3)):
            for half in range(2):
                at = pl.multiple_of(half * ROWS + sub * SUB, 16)
                copies.append(
                    pltpu.make_async_copy(
                        a.at[pl.ds(at, SUB)], out_ref.at[n, half], sems.at[d, n, half]
                    )
                )
    for copy in copies:
        copy.start()
    for copy in copies:
        copy.wait()


def pack(arrived):
    return pl.pallas_call(
        pack_kernel,
        in_specs=[pl.BlockSpec(memory_space=pl.ANY)] * NX,
        out_specs=[VMEM] * NY,
        out_shape=[jax.ShapeDtypeStruct((NX, 2, SUB, WIDTH), BF)] * NY,
        scratch_shapes=[pltpu.SemaphoreType.DMA((NY, NX, 2))],
        compiler_params=pltpu.CompilerParams(vmem_limit_bytes=4 << 20),
        cost_estimate=pl.CostEstimate(flops=1, bytes_accessed=40_000_000, transcendentals=0),
        name="pack",
    )(*arrived)


def out_kernel(p0, p1, p2, p3, own_ref, w_ref, gate_ref, mine_ref, other_ref, rows):
    y = lax.axis_index("tm") % NY
    for half in range(2):
        for d in range(NX):
            part = [p[d, half] for p in (p0, p1, p2, p3)]
            at = slice(half * ROWS, (half + 1) * ROWS)
            rows[at, d * WIDTH : (d + 1) * WIDTH] = jnp.concatenate(part, axis=0)
    for n in range(NY):
        cols = slice(n * COLS, (n + 1) * COLS)
        block = [own_ref[:, cols]]
        block += [w_ref[z, n, d] for d in range(NX - 1) for z in range(NZ)]
        block = jnp.concatenate(block, axis=0)
        proj = jnp.dot(rows[...], block, preferred_element_type=F32)
        for d in range(NY):
            gate = gate_ref[pl.ds((y - d) % NY, 1), cols]
            mine_ref[n, d] = (proj[d * SUB : (d + 1) * SUB] * gate).astype(BF)
            other_ref[n, d] = (proj[ROWS + d * SUB : ROWS + (d + 1) * SUB] * gate).astype(BF)


def out_project(pieces, own, gathered, gates):
    return pl.pallas_call(
        out_kernel,
        in_specs=[VMEM] * 7,
        out_specs=[VMEM] * 2,
        out_shape=[jax.ShapeDtypeStruct((NY, NY, SUB, COLS), BF)] * 2,
        scratch_shapes=[pltpu.VMEM((2 * ROWS, NX * WIDTH), BF)],
        compiler_params=pltpu.CompilerParams(vmem_limit_bytes=12 << 20),
        cost_estimate=pl.CostEstimate(
            flops=4 * ROWS * NX * WIDTH * D, bytes_accessed=12_000_000, transcendentals=0
        ),
        name="out_project",
    )(*pieces, own, gathered, gates)


def row_kernel(part, own_ref, other_ref, part_ref, total_ref, held):
    y = lax.axis_index("tm") % NY
    for n in range(PER):
        for d in range(NY):
            at = PER * part + n
            held[(y - d) % NY] = own_ref[at, d].astype(F32) + other_ref[at, d].astype(F32)
        held[1] = held[0] + held[1]
        held[2] = held[1] + held[2]
        held[3] = held[2] + held[3]
        total_ref[n] = held[3].astype(BF)
        for d in range(NY):
            part_ref[d, n] = held[(y - d) % NY]


def row_prefix(part, own, other):
    return pl.pallas_call(
        functools.partial(row_kernel, part),
        in_specs=[VMEM] * 2,
        out_specs=[VMEM] * 2,
        out_shape=[
            jax.ShapeDtypeStruct((NY, PER, SUB, COLS), F32),
            jax.ShapeDtypeStruct((PER, SUB, COLS), BF),
        ],
        scratch_shapes=[pltpu.VMEM((NY, SUB, COLS), F32)],
        compiler_params=pltpu.CompilerParams(vmem_limit_bytes=12 << 20),
        cost_estimate=pl.CostEstimate(flops=1, bytes_accessed=2_000_000, transcendentals=0),
        name="row_prefix",
    )(own, other)


def final_kernel(lat_ref, *refs):
    pieces, firsts, out_ref = refs[:4], refs[4:8], refs[-1]
    step = lax.axis_index("tm")
    y = step % NY
    for d in range(NY):
        at = (y + d) % NY
        first = jnp.where(step == 0, lat_ref[at], firsts[d][...])
        out_ref[at] = first + pieces[d][0].astype(F32)


def final_sum(part, latents, pieces, firsts, earlier):
    piece = pl.BlockSpec((1, SUB, COLS), lambda n: (n, 0, 0))
    first = pl.BlockSpec((SUB, COLS), lambda n: (0, PER * part + n))
    block = pl.BlockSpec((NY, SUB, COLS), lambda n: (0, 0, PER * part + n))
    more = [] if earlier is None else [earlier]
    return pl.pallas_call(
        final_kernel,
        grid=(PER,),
        in_specs=[block] + [piece] * 4 + [first] * 4 + [pl.BlockSpec(memory_space=pl.ANY)] * len(more),
        out_specs=block,
        out_shape=jax.ShapeDtypeStruct((NY, SUB, D), F32),
        input_output_aliases={9: 0} if more else {},
        compiler_params=pltpu.CompilerParams(vmem_limit_bytes=12 << 20),
        cost_estimate=pl.CostEstimate(flops=1, bytes_accessed=1, transcendentals=0),
        name="final_sum",
    )(latents.reshape(NY, SUB, D), *pieces, *firsts, *more)


def barrier(*arrays):
    return lax.optimization_barrier(arrays)


def per_device(latents, timesteps, mod_weight, qkv_weight, qk_gain, out_weight, block_list):
    step = lax.axis_index("tm")
    z, y = step // NY, step % NY

    piece = lax.dynamic_slice(out_weight, (z * DEEP, y * COLS), (DEEP, COLS))
    pieces = [shift_x(piece, d) for d in range(1, NX)]
    first_core = lax.axis_index("seq") % 2 == 0
    y_is = [y == n for n in range(NY)]
    z_is = [z == n for n in range(NZ)]
    z_from = [z >= n for n in range(NZ)]
    z_odd = z % 2 == 1
    modulated = modulate(latents, timesteps, mod_weight)
    modulated, pieces, first_core, y_is, z_is, z_from, z_odd = barrier(
        modulated, pieces, first_core, y_is, z_is, z_from, z_odd
    )
    gathered = lax.all_gather(jnp.stack(pieces), "tm").reshape(NZ, NY, NX - 1, DEEP, COLS)

    twin = swap_core(modulated)
    before = shift_x(modulated, 1)
    after = shift_x(modulated, -1)

    twin, current, weight, gate_weight = barrier(twin, latents[0], qkv_weight, mod_weight)
    gates = row_gates(timesteps, gate_weight)
    half = current.astype(jnp.float16).reshape(NY, SUB, D)
    parts = [shift_y(half[to], to) for to in range(1, NY)]
    held = qkv_tiles([modulated, twin], ((0, 0), (0, 1)), qk_gain, weight, None)

    before, after, held, parts, half, gates = barrier(before, after, held, parts, half, gates)
    far = opposite_x(first_core, before, after)
    quarter = half[0]
    for to in range(1, NY):
        quarter = jnp.where(y_is[to], parts[to - 1], quarter)
    got = shift_z(quarter, 2)
    near = [after, swap_core(after), before, swap_core(before)]
    places = ((1, 0), (1, 1), (3, 0), (3, 1))
    held = qkv_tiles(near, places, qk_gain, weight, held)
    far, held, quarter, got = barrier(far, held, quarter, got)
    quarter = jnp.where(z_is[2], got, quarter)
    held = qkv_tiles([far, swap_core(far)], ((2, 0), (2, 1)), qk_gain, weight, held)

    arrived = [None] * NX
    for d in (2, 1, 3, 0):
        if d == 0:
            held, arrived[2], quarter = barrier(held, arrived[2], quarter)
            got = shift_z(quarter, 1)
        attended = attend_tile(block_list, d, held)
        arrived[d] = shift_x(attended, d) if d else attended

    arrived, gathered, own_weight = barrier(arrived, gathered, out_weight)
    pieces = pack(arrived)
    pieces = [shift_y(send, d) if d else send for d, send in enumerate(pieces)]
    own_weight, gathered = load(own_weight, gathered)

    pieces[1], got, quarter = barrier(pieces[1], got, quarter)
    quarter = jnp.where(z_odd, got, quarter)
    firsts = [shift_y(quarter, -d) if d else quarter for d in range(NY)]
    own, other = out_project(pieces, own_weight, gathered, gates)
    other = swap_core(other)

    result = None
    for part in range(PARTS):
        parts, total = row_prefix(part, own, other)
        base = sum(
            jnp.where(z_from[by], shift_z(total, by).astype(F32), 0.0) for by in range(1, NZ)
        )
        back = []
        for d in range(NY):
            send = (parts[d] + base).astype(BF)
            back.append(shift_y(send, -d) if d else send)
        if part == 0:
            firsts = [first.astype(F32) for first in firsts]
        result = final_sum(part, latents, back, firsts, result)
    return result.reshape(1, ROWS, D)


def solution(mesh):
    return jax.shard_map(
        per_device,
        mesh=mesh,
        in_specs=(
            P("tm", "seq", None),
            P(),
            P(),
            P(None, None, "seq"),
            P(),
            P("seq", None),
            P("seq", None, None),
        ),
        out_specs=P("tm", "seq", None),
        check_vma=False,
    )
```
